256 devices in a mesh: dp: 16 (over z_lo, x), fsdp: 16 (over y, z_hi, core).
Axes of the slice: x: 4, y: 4, z: 8 (z_hi: 2, z_lo: 4; z = z_hi * 4 + z_lo), core: 2. Of those that a mesh axis runs over, the one named last changes fastest.
Arguments:
- hidden: bfloat16 [131072, 4096], P(('dp', 'fsdp')), may hold values from -6 to 6
- temporal_gain: float32 [4096], replicated, may hold values from 0.1 to 1.9
- in_weight: bfloat16 [4096, 1024], P('fsdp'), may hold values from -0.09375 to 0.09375
- in_scale: bfloat16 [4096], P('fsdp'), may hold values from 0.25 to 4
- depth_gain: float32 [1024], replicated, may hold values from 0.1 to 1.9
- head_weight: bfloat16 [4, 1024, 1024], P(None, 'fsdp'), may hold values from -0.625 to 0.625
- code_ids: int32 [131072, 4], P(('dp', 'fsdp')), may hold values from 0 to 1023
Outputs:
- frame_loss: float32 [131072, 4], P(('dp', 'fsdp'))
- head_grad: float32 [4, 1024, 1024], P(None, 'fsdp')
The draws below stay inside these ranges and needn't reach their ends.
All inputs are finite; a program needn't handle non-finite values.
Results may differ from the reference program's by a relative error of at most 0.0043.
Values may be sent and summed in bfloat16 or wider, within the bound.
A program may use at most 128 MiB of HBM per device.

```python
import math
import jax
import jax.numpy as jnp
import numpy as np
from jax import lax

D = 4096
DD = 1024
K = 4
CARD = 1024
TOKENS = 131072


def touch_ends(drawn, stream_key, low, top_value):
    longest = drawn.shape.index(max(drawn.shape))
    spots = []
    for shift in (0, 1):
        where = [jax.random.randint(jax.random.fold_in(stream_key, axis), (), 0, length) for axis, length in enumerate(drawn.shape)]
        where[longest] = (where[longest] + shift) % drawn.shape[longest]
        spots.append(tuple(where))
    return drawn.at[spots[0]].set(low).at[spots[1]].set(top_value)


def shard_levels(stream_key, dims, shards, smallest, high):
    gain, own = 1.0, jax.random.fold_in(stream_key, 6)
    for axis_at, parts in shards:
        draws = jnp.exp(jax.random.uniform(jax.random.fold_in(own, axis_at), (parts,), jnp.float32, smallest / len(shards), high / len(shards)))
        gain = gain * jnp.repeat(draws, dims[axis_at] // parts).reshape([-1 if axis == axis_at else 1 for axis in range(len(dims))])
    return gain


def cumulative_ranks(amount, slope):
    loads = [(1 << 20) // math.isqrt(rank ** slope) + 1 for rank in range(1, amount + 1)]
    width = 1 + sum(loads) // (1 << 30)
    return np.cumsum(np.array([max(1, weight // width) for weight in loads]))


def ranked(rng, dims, count, lean):
    table = cumulative_ranks(count, lean)
    lot = jax.random.randint(jax.random.fold_in(rng, 1), dims, 0, int(table[count - 1]))
    rank = jnp.searchsorted(jnp.asarray(table, jnp.int32), lot, side="right")
    return jax.random.permutation(jax.random.fold_in(rng, 2), count)[rank].astype(jnp.int32)


def gaussian(rng, dims, deviation, bound, shards=(), held_as=jnp.bfloat16):
    factor_of = shard_levels(rng, dims, shards, -0.22, 0.18) if shards else 1.0
    result = jax.random.normal(rng, dims, jnp.float32) * deviation * factor_of
    return jnp.minimum(jnp.maximum(result, -bound), bound).astype(held_as)


def setup_inputs(seed: int = 0) -> dict:
    arg_keys = jax.random.split(jax.random.key(seed), 8)
    return {
        "hidden": gaussian(arg_keys[0], (TOKENS, D), 1.0, 6.0, ((0, 256),)),
        "temporal_gain": jnp.clip(1.0 + 0.18 * jax.random.normal(arg_keys[1], (D,), jnp.float32), 0.1, 1.9),
        "in_weight": gaussian(arg_keys[2], (D, DD), D ** -0.5, 0.09375, ((0, 16),)),
        "in_scale": jnp.clip(jnp.exp(math.log(4.0) - 2.7725887 * jax.random.uniform(arg_keys[3], (D,), jnp.float32) ** shard_levels(arg_keys[3], (D,), ((0, 16),), -0.2, 0.2)), 0.25, 4.0).astype(jnp.bfloat16),
        "depth_gain": jnp.clip(1.0 + 0.18 * jax.random.normal(arg_keys[4], (DD,), jnp.float32), 0.1, 1.9),
        "head_weight": gaussian(arg_keys[5], (K, CARD, DD), (DD // 12) ** -0.5, 0.625, ((1, 16),)),
        "code_ids": touch_ends(ranked(arg_keys[6], (TOKENS, K), CARD, 1), jax.random.fold_in(arg_keys[6], 3), 0, CARD - 1).astype(jnp.int32),
    }


epsilon = 1e-05
softcap = 30.0
loss_scale = 0.0625

def reference(hidden, temporal_gain, in_weight, in_scale, depth_gain, head_weight, code_ids):
    weight = (in_weight.astype(jnp.float32) * in_scale.astype(jnp.float32)[:, None]).astype(jnp.bfloat16)
    block_rows = math.gcd(TOKENS, 4096)
    heads_wide = head_weight.astype(jnp.float32)

    def block_step(accum, index_now):
        first_row = (index_now * block_rows).astype(jnp.int32)
        row_block = lax.dynamic_slice_in_dim(hidden, first_row, block_rows, 0).astype(jnp.float32)
        block_ids = lax.dynamic_slice_in_dim(code_ids, first_row, block_rows, 0)
        normed = (row_block * lax.rsqrt(lax.optimization_barrier(jnp.mean(row_block * row_block, axis=-1, keepdims=True)) + epsilon) * temporal_gain).astype(jnp.bfloat16)
        depth_in = jnp.dot(normed, weight, preferred_element_type=jnp.float32)
        depth_rows = (depth_in * lax.rsqrt(lax.optimization_barrier(jnp.mean(depth_in * depth_in, axis=-1, keepdims=True)) + epsilon) * depth_gain).astype(jnp.bfloat16)
        scores = jnp.einsum('rd,kcd->rkc', depth_rows.astype(jnp.float32), heads_wide)
        capped = softcap * jnp.tanh(scores / softcap)
        log_total = jnp.log(lax.optimization_barrier(jnp.sum(jnp.exp(capped), axis=2)))
        target = jnp.take_along_axis(capped, block_ids[:, :, None], axis=2)[:, :, 0]
        onehot = (block_ids[:, :, None] == jnp.arange(CARD, dtype=jnp.int32)[None, None, :]).astype(jnp.float32)
        prob_rows = jnp.exp(capped - log_total[:, :, None])
        dlogits = ((prob_rows - onehot) * (1.0 - (capped / softcap) ** 2) * loss_scale).astype(jnp.bfloat16)
        accum = accum + jnp.einsum('rkc,rd->kcd', dlogits.astype(jnp.float32), depth_rows.astype(jnp.float32))
        return (accum, log_total - target)
    start_grad = jnp.zeros((K, CARD, DD), jnp.float32)
    head_grad, losses = lax.scan(block_step, start_grad, jnp.arange(TOKENS // block_rows, dtype=jnp.int32))
    return (losses.reshape(TOKENS, K), head_grad)
```

```python
import functools

import jax
import jax.numpy as jnp
from jax import lax
from jax.experimental import pallas as pl
from jax.experimental.pallas import tpu as pltpu
from jax.sharding import PartitionSpec as P

MESH = pl.DeviceIdType.MESH
f32, bf16 = jnp.float32, jnp.bfloat16
eps = 1e-05
cap = 30.0
loss_scale = 0.0625

Y_A, Y_B, Y_C, Y2, ZU, ZD, XQ = 0, 2, 4, 6, 8, 12, 16
GATHER = 26
SIB_W, SIB_R, SIB_S, SIB_I = 52, 60, 61, 62
A2, A1M, A1A, B2, B1M, B1A, S2A, S2B, S3, GZ, GX = 63, 71, 79, 87, 89, 91, 93, 96, 99, 106, 109
N_SEM = 112


def kernel(
    hidden, t_gain, weight, scale, d_gain, heads, ids,
    loss_out, grad_out,
    hid, normed, wg, hg, acc, rows, tb, eb, dl, gb,
    ra2, ra1m, ra1a, saa, rb2, rb1m, rb1a, sab, sa, sb, s2a, r2a, s2b, r2b, tt, s3, r3, fin,
    idb, sums, lsem, ss, rs,
):
    dp, fs = lax.axis_index("dp"), lax.axis_index("fsdp")
    x, y, c = dp % 4, fs // 4, fs % 2
    h, j = (fs // 2) % 2, dp // 4
    z = h * 4 + j
    par = x % 2

    def dev(px, py, pz, pc=None):
        px, py, pz = (px + 4) % 4, (py + 4) % 4, (pz + 8) % 8
        return {"dp": (pz % 4) * 4 + px, "fsdp": (py * 2 + pz // 4) * 2 + (c if pc is None else pc)}

    sib = dev(x, y, z, 1 - c)
    xd = lambda d: dev(x + d, y, z)
    yd = lambda d: dev(x, y + d, z)
    zd = lambda d: dev(x, y, z + d)

    def copy(src, dst, sem, to):
        return pltpu.make_async_remote_copy(
            src_ref=src, dst_ref=dst, send_sem=ss.at[sem], recv_sem=rs.at[sem], device_id=to, device_id_type=MESH
        )

    hid_copy = pltpu.make_async_copy(hidden, hid, lsem.at[0])
    hid_copy.start()
    own = y * 2 + h
    head_copy = pltpu.make_async_copy(heads, hg.at[own], lsem.at[1])
    head_copy.start()

    barrier = pltpu.get_barrier_semaphore()
    everyone = [sib] + [xd(d) for d in (1, 2, 3)] + [yd(d) for d in (1, 2, 3)] + [zd(d) for d in range(1, 8)]
    for to in everyone:
        pl.semaphore_signal(barrier, inc=1, device_id=to, device_id_type=MESH)

    mine = pl.ds(pl.multiple_of(c * 256, 256), 256)
    wg[own, mine, :] = (weight[...].astype(f32) * scale[...].astype(f32)).astype(bf16)
    idb[pl.ds(c, 1)] = ids[...][None]
    pl.semaphore_wait(barrier, len(everyone))

    def slot(role):
        off = jnp.where(role % 4 == 1, 3, jnp.where(role % 4 == 2, 1, jnp.where(role % 4 == 3, 2, 0)))
        return ((y + off) % 4) * 2 + jnp.where(role < 4, h, 1 - h)

    def piece(m, role, start, count):
        if m == 0:
            return wg.at[slot(role), pl.ds(pl.multiple_of(c * 256 + start, 64), count)]
        return hg.at[slot(role), pl.ds(pl.multiple_of(start, 64), count)]

    q0, q1, rest = par * 128, par * 128 + 64, (1 - par) * 128
    o0, o1 = (1 - par) * 128, (1 - par) * 128 + 64

    def move(m, role, start, count, sem, to):
        ref = piece(m, role, start, count)
        return copy(ref, ref, m * GATHER + sem, to)

    def y_sends(m):
        for sem, plus, minus, count in ((Y_A, q0, q1, 64), (Y_B, q1, q0, 64), (Y_C, rest, rest, 128)):
            move(m, 0, plus, count, sem, yd(1)).start()
            move(m, 0, minus, count, sem + 1, yd(-1)).start()

    def z_source(m, k):
        @pl.when(j == 3)
        def _():
            move(m, k, q0, 64, ZU + k, zd(1)).start()

        @pl.when(j == 0)
        def _():
            move(m, k, q1, 64, ZD + k, zd(-1)).start()

    def y_quarters(m):
        move(m, 1, q0, 64, Y_A, yd(1)).wait_recv()
        move(m, 1, q0, 64, Y2, yd(1)).start()
        move(m, 2, q1, 64, Y_A + 1, yd(-1)).wait_recv()
        move(m, 2, q1, 64, Y2 + 1, yd(-1)).start()
        move(m, 1, q1, 64, Y_B, yd(1)).wait_recv()
        z_source(m, 1)
        move(m, 2, q0, 64, Y_B + 1, yd(-1)).wait_recv()
        z_source(m, 2)

    def y_rest(m):
        move(m, 1, rest, 128, Y_C, yd(1)).wait_recv()
        move(m, 2, rest, 128, Y_C + 1, yd(-1)).wait_recv()

    def x_sends(m, role):
        move(m, role, q0, 64, XQ + 2 * (role - 3), xd(1)).start()
        move(m, role, q1, 64, XQ + 2 * (role - 3) + 1, xd(-1)).start()

    def y_far(m):
        move(m, 3, q0, 64, Y2, yd(1)).wait_recv()
        move(m, 3, q1, 64, Y2 + 1, yd(-1)).wait_recv()
        x_sends(m, 3)
        z_source(m, 3)

    def z_pass(m, k):
        move(m, 4 + k, q0, 64, ZU + k, zd(1)).wait_recv()

        @pl.when(j < 3)
        def _():
            move(m, 4 + k, q0, 64, ZU + k, zd(1)).start()

        move(m, 4 + k, q1, 64, ZD + k, zd(-1)).wait_recv()

        @pl.when(j > 0)
        def _():
            move(m, 4 + k, q1, 64, ZD + k, zd(-1)).start()

        x_sends(m, 4 + k)

    def x_wait(m, role):
        sem = XQ + 2 * (role - 3)
        move(m, role, o0, 64, sem, xd(1)).wait_recv()
        move(m, role, o1, 64, sem + 1, xd(-1)).wait_recv()

    def to_sibling(role):
        ref = wg.at[slot(role), mine]
        return copy(ref, ref, SIB_W + role, sib)

    theirs = pl.ds(pl.multiple_of((1 - c) * 256, 256), 256)

    def project(role):
        ref = wg.at[slot(role), theirs]
        copy(ref, ref, SIB_W + role, sib).wait_recv()
        s = slot(role)

        @pl.loop(0, 4)
        def _(n):
            cols = pl.ds(pl.multiple_of(n * 256, 256), 256)
            acc[:, cols] += jnp.dot(normed[s], wg[s, :, cols], preferred_element_type=f32)

    to_sibling(0).start()
    y_sends(0)
    z_source(0, 0)
    id_copy = copy(idb.at[c], idb.at[c], SIB_I, sib)
    id_copy.start()
    hid_copy.wait()
    head_copy.wait()
    y_sends(1)
    z_source(1, 0)

    @pl.loop(0, 32)
    def _(r):
        at = pl.ds(pl.multiple_of(r * 16, 16), 16)
        block = hid[at, :].astype(f32)
        inv = lax.rsqrt(jnp.mean(block * block, axis=-1, keepdims=True) + eps)
        out = (block * inv * t_gain[...]).astype(bf16)
        for s in range(8):
            normed[s, at, :] = out[:, s * 512 : (s + 1) * 512]

    acc[...] = jnp.zeros_like(acc)
    y_quarters(0)
    z_pass(0, 0)
    y_far(0)
    y_quarters(1)
    z_pass(1, 0)
    z_pass(0, 1)
    z_pass(0, 2)
    y_far(1)
    y_rest(0)
    to_sibling(1).start()
    to_sibling(2).start()
    z_pass(0, 3)
    project(0)
    z_pass(1, 1)
    z_pass(1, 2)
    project(1)
    project(2)
    x_wait(0, 3)
    to_sibling(3).start()
    x_wait(0, 4)
    to_sibling(4).start()
    z_pass(1, 3)
    project(3)
    x_wait(0, 5)
    to_sibling(5).start()
    project(4)
    x_wait(0, 6)
    to_sibling(6).start()
    project(5)
    x_wait(0, 7)
    to_sibling(7).start()
    project(6)
    project(7)

    @pl.loop(0, 16)
    def _(r):
        at = pl.ds(pl.multiple_of(r * 32, 32), 32)
        block = acc[at, :]
        inv = lax.rsqrt(jnp.mean(block * block, axis=-1, keepdims=True) + eps)
        rows[pl.ds(pl.multiple_of(c * 512 + r * 32, 32), 32), :] = (block * inv * d_gain[...]).astype(bf16)

    my_rows = rows.at[pl.ds(pl.multiple_of(c * 512, 512), 512)]
    row_copy = copy(my_rows, my_rows, SIB_R, sib)
    sums[...] = jnp.zeros_like(sums)
    row_copy.start()
    id_copy.wait_recv()
    row_copy.wait_recv()
    y_rest(1)

    def score(role):
        s = slot(role)

        @pl.loop(0, 4)
        def _(n):
            cols = pl.ds(pl.multiple_of(n * 256, 256), 256)
            got = lax.dot_general(
                hg[s], rows[cols, :], (((1,), (1,)), ((), ())), preferred_element_type=f32
            )
            t = jnp.tanh(got * (1.0 / cap))
            e = jnp.exp(t * cap)
            tb[s, :, cols] = t
            eb[s, :, cols] = e
            ids_at = idb[n // 2, :, pl.ds(pl.multiple_of((n % 2) * 256, 256), 256)]
            card = lax.broadcasted_iota(jnp.int32, (64, 256), 0) + (s * 2 + c) * 64
            for k in range(4):
                part = slice(k * 64, (k + 1) * 64)
                hit = card == ids_at[k : k + 1, :]
                sums[c, k : k + 1, cols] += jnp.sum(e[part], axis=0, keepdims=True)
                sums[c, k + 4 : k + 5, cols] += jnp.sum(jnp.where(hit, t[part], 0.0), axis=0, keepdims=True)

    @pl.loop(0, 3)
    def _(role):
        score(role)

    @pl.loop(3, 8)
    def _(role):
        x_wait(1, role)
        score(role)

    my_sums = sums.at[c]
    sum_copy = copy(my_sums, my_sums, SIB_S, sib)
    sum_copy.start()
    sum_copy.wait_recv()
    totals = sums[0, 0:4, :] + sums[1, 0:4, :]
    mine_f = pl.ds(pl.multiple_of(c * 512, 512), 512)
    loss_out[...] = jnp.log(sums[0, 0:4, mine_f] + sums[1, 0:4, mine_f]) - cap * (
        sums[0, 4:8, mine_f] + sums[1, 4:8, mine_f]
    )
    sum_copy.wait_send()
    sums[c, 0:4, :] = 1.0 / totals

    def gradient(i):
        hp = i % 2
        s = 1 - 2 * hp
        step = i // 2
        off = jnp.where(step == 0, 2, jnp.where(step == 1, 4 - s, jnp.where(step == 2, 4 + s, 0)))
        b = ((y + off) % 4) * 2 + hp

        @pl.loop(0, 4)
        def _(n):
            cols = pl.ds(pl.multiple_of(n * 256, 256), 256)
            ids_at = idb[n // 2, :, pl.ds(pl.multiple_of((n % 2) * 256, 256), 256)]
            card = lax.broadcasted_iota(jnp.int32, (64, 256), 0) + (b * 2 + c) * 64
            for k in range(4):
                part = slice(k * 64, (k + 1) * 64)
                t = tb[b, part, cols]
                p = eb[b, part, cols] * sums[c, k : k + 1, cols]
                hit = card == ids_at[k : k + 1, :]
                p = jnp.where(hit, p - 1.0, p)
                dl[part, cols] = (p * ((1.0 - t * t) * loss_scale)).astype(bf16)

        @pl.loop(0, 4)
        def _(n):
            cols = pl.ds(pl.multiple_of(n * 256, 256), 256)
            g = jnp.dot(dl[...], rows[:, cols], preferred_element_type=f32)
            eb[b, :, cols] = g
            gb[b, :, cols] = g.astype(bf16)

        head = lambda d: pl.ds(pl.multiple_of(((x + d + 4) % 4) * 64, 64), 64)
        copy(gb.at[b, head(2), pl.ds(0, 512)], ra2.at[b], A2 + b, xd(s)).start()
        copy(gb.at[b, head(-s), pl.ds(0, 512)], ra1m.at[b], A1M + b, xd(-s)).start()

        @pl.when(step == 0)
        def _():
            copy(gb.at[b, :, pl.ds(512, 512)], rb2.at[hp], B2 + hp, yd(s)).start()

        @pl.when(step == 1)
        def _():
            copy(gb.at[b, :, pl.ds(512, 512)], rb1m.at[hp], B1M + hp, yd(-s)).start()

    @pl.loop(0, 8)
    def _(i):
        gradient(i)

    for hp in range(2):
        s = 1 - 2 * hp
        b = ((y + s + 4) % 4) * 2 + hp
        copy(sab.at[hp], rb2.at[hp], B2 + hp, yd(s)).wait_recv()
        for r in range(4):
            part = slice(r * 64, (r + 1) * 64)
            sab[hp, part, :] = (eb[b, part, 512:1024] + rb2[hp, part, :].astype(f32)).astype(bf16)
        copy(sab.at[hp], rb1a.at[hp], B1A + hp, yd(s)).start()

    @pl.loop(0, 8)
    def _(b):
        s = 1 - 2 * (b % 2)
        at = pl.ds(pl.multiple_of(((x + s + 4) % 4) * 64, 64), 64)
        copy(saa.at[b], ra2.at[b], A2 + b, xd(s)).wait_recv()
        saa[b] = (eb[b, at, 0:512] + ra2[b].astype(f32)).astype(bf16)
        copy(saa.at[b], ra1a.at[b], A1A + b, xd(s)).start()

    my_head = pl.ds(pl.multiple_of(x * 64, 64), 64)
    for hp in range(2):
        s = 1 - 2 * hp
        copy(sab.at[hp], rb1m.at[hp], B1M + hp, yd(-s)).wait_recv()
        copy(sab.at[hp], rb1a.at[hp], B1A + hp, yd(s)).wait_recv()
        for r in range(4):
            part = slice(r * 64, (r + 1) * 64)
            sb[hp, part, :] = (
                eb[y * 2 + hp, part, 512:1024] + rb1m[hp, part, :].astype(f32) + rb1a[hp, part, :].astype(f32)
            )
    for d in (2, 1, 3):
        at = pl.ds(pl.multiple_of(((x + d) % 4) * 64, 64), 64)
        s2b[d - 1] = sb[:, at, :].astype(bf16)
        copy(s2b.at[d - 1], r2b.at[d - 1], S2B + d - 1, xd(d)).start()

    @pl.loop(0, 8)
    def _(b):
        s = 1 - 2 * (b % 2)
        copy(saa.at[b], ra1m.at[b], A1M + b, xd(-s)).wait_recv()
        copy(saa.at[b], ra1a.at[b], A1A + b, xd(s)).wait_recv()
        sa[b] = eb[b, my_head, 0:512] + ra1m[b].astype(f32) + ra1a[b].astype(f32)

    for d in (2, 1, 3):
        s2a[d - 1] = sa[pl.ds(((y + d) % 4) * 2, 2)].astype(bf16)
        copy(s2a.at[d - 1], r2a.at[d - 1], S2A + d - 1, yd(d)).start()

    for d in range(3):
        copy(s2b.at[d], r2b.at[d], S2B + d, xd(d + 1)).wait_recv()
    tt[:, :, 512:1024] = (
        sb[:, my_head, :] + r2b[0].astype(f32) + r2b[1].astype(f32) + r2b[2].astype(f32)
    )
    for d in range(3):
        copy(s2a.at[d], r2a.at[d], S2A + d, yd(d + 1)).wait_recv()
    tt[:, :, 0:512] = (
        sa[pl.ds(y * 2, 2)] + r2a[0].astype(f32) + r2a[1].astype(f32) + r2a[2].astype(f32)
    )
    s3[...] = tt[...].astype(bf16)
    for d in (4, 3, 5, 2, 6, 1, 7):
        to = (z + d) % 8
        at = pl.ds(pl.multiple_of((to % 4) * 16, 16), 16)
        copy(s3.at[to // 4, at], r3.at[d - 1], S3 + d - 1, zd(d)).start()
    strip = pl.ds(pl.multiple_of(j * 16, 16), 16)
    total = tt[h, strip, :]
    for d in (1, 7, 2, 6, 3, 5, 4):
        copy(r3.at[d - 1], r3.at[d - 1], S3 + d - 1, zd(d)).wait_recv()
        total = total + r3[d - 1].astype(f32)

    fin[x, strip, :] = total.astype(bf16)
    def z_share(d):
        to = h * 4 + (j + d) % 4
        return copy(fin.at[x, strip], fin.at[x, strip], GZ + d - 1, dev(x, y, to))
    for d in (2, 1, 3):
        z_share(d).start()
    for d in (1, 2, 3):
        z_share(d).wait_recv()
    def x_share(d):
        return copy(fin.at[x], fin.at[x], GX + d - 1, xd(d))
    for d in (2, 1, 3):
        x_share(d).start()
    grad_out[x] = fin[x].astype(f32)
    for d in (1, 3, 2):
        x_share(d).wait_recv()
        src = (x + 4 - d) % 4
        grad_out[src] = fin[src].astype(f32)

    for m in range(2):
        for sem, count in ((Y_A, 64), (Y_A + 1, 64), (Y_B, 64), (Y_B + 1, 64), (Y_C, 128), (Y_C + 1, 128)):
            move(m, 0, 0, count, sem, yd(1)).wait_send()
        for sem in range(Y2, GATHER):
            move(m, 0, 0, 64, sem, yd(1)).wait_send()
    for role in range(8):
        to_sibling(role).wait_send()
    row_copy.wait_send()
    id_copy.wait_send()
    for b in range(8):
        for sem in (A2, A1M, A1A):
            copy(saa.at[b], ra2.at[b], sem + b, sib).wait_send()
    for hp in range(2):
        for sem in (B2, B1M, B1A):
            copy(sab.at[hp], rb2.at[hp], sem + hp, sib).wait_send()
    for d in range(3):
        copy(s2a.at[d], r2a.at[d], S2A + d, sib).wait_send()
        copy(s2b.at[d], r2b.at[d], S2B + d, sib).wait_send()
        z_share(d + 1).wait_send()
        x_share(d + 1).wait_send()
    for d in range(7):
        copy(r3.at[d], r3.at[d], S3 + d, sib).wait_send()


def shards(hidden, temporal_gain, in_weight, in_scale, depth_gain, head_weight, code_ids):
    vmem = pl.BlockSpec(memory_space=pltpu.VMEM)
    hbm = pl.BlockSpec(memory_space=pl.ANY)
    V = pltpu.VMEM
    loss, grad = pl.pallas_call(
        kernel,
        out_shape=(jax.ShapeDtypeStruct((4, 512), f32), jax.ShapeDtypeStruct((4, 64, 1024), f32)),
        in_specs=[hbm, vmem, vmem, vmem, vmem, hbm, vmem],
        out_specs=(vmem, vmem),
        scratch_shapes=[
            V((512, 4096), bf16), V((8, 512, 512), bf16), V((8, 512, 1024), bf16), V((8, 256, 1024), bf16),
            V((512, 1024), f32), V((1024, 1024), bf16), V((8, 256, 1024), f32), V((8, 256, 1024), f32),
            V((256, 1024), bf16), V((8, 256, 1024), bf16),
            V((8, 64, 512), bf16), V((8, 64, 512), bf16), V((8, 64, 512), bf16), V((8, 64, 512), bf16),
            V((2, 256, 512), bf16), V((2, 256, 512), bf16), V((2, 256, 512), bf16), V((2, 256, 512), bf16),
            V((8, 64, 512), f32), V((2, 256, 512), f32),
            V((3, 2, 64, 512), bf16), V((3, 2, 64, 512), bf16), V((3, 2, 64, 512), bf16), V((3, 2, 64, 512), bf16),
            V((2, 64, 1024), f32), V((2, 64, 1024), bf16), V((7, 16, 1024), bf16), V((4, 64, 1024), bf16),
            V((2, 4, 512), jnp.int32), V((2, 8, 1024), f32),
            pltpu.SemaphoreType.DMA((2,)), pltpu.SemaphoreType.DMA((N_SEM,)), pltpu.SemaphoreType.DMA((N_SEM,)),
        ],
        compiler_params=pltpu.CompilerParams(
            collective_id=0, has_side_effects=True, vmem_limit_bytes=63 * 2**20
        ),
    )(
        hidden, temporal_gain[None, :], in_weight, in_scale[:, None], depth_gain[None, :],
        head_weight.reshape(256, 1024), code_ids.T,
    )
    return loss.T, grad


def solution(mesh):
    in_specs = (
        P(("dp", "fsdp"), None),
        P(),
        P("fsdp", None),
        P("fsdp"),
        P(),
        P(None, "fsdp", None),
        P(("dp", "fsdp"), None),
    )
    out_specs = (P(("dp", "fsdp"), None), P(None, "fsdp", None))
    return jax.shard_map(shards, mesh=mesh, in_specs=in_specs, out_specs=out_specs, check_vma=False)
```

```python
import functools

import jax
import jax.numpy as jnp
from jax import lax
from jax.experimental import pallas as pl
from jax.experimental.pallas import tpu as pltpu
from jax.sharding import PartitionSpec as P

MESH = pl.DeviceIdType.MESH
f32, bf16 = jnp.float32, jnp.bfloat16
eps = 1e-05
cap = 30.0
loss_scale = 0.0625

Y_A, Y_B, Y_C, Y2, ZU, ZD, XQ = 0, 2, 4, 6, 8, 12, 16
GATHER = 26
SIB_W, SIB_R, SIB_S, SIB_I = 52, 60, 61, 62
A2, A1M, A1A, B2, B1M, B1A, S2A, S2B, S3, GZ, GX = 63, 71, 79, 87, 89, 91, 93, 96, 99, 106, 109
N_SEM = 112


def kernel(
    hidden, t_gain, weight, scale, d_gain, heads, ids,
    loss_out, grad_out,
    hid, normed, pg, ws, acc, rows, tb, eb, dl, gb,
    ra2, ra1m, ra1a, saa, rb2, rb1m, rb1a, sab, sa, sb, s2a, r2a, s2b, r2b, tt, s3, r3, fin,
    idb, sums, lsem, ss, rs,
):
    dp, fs = lax.axis_index("dp"), lax.axis_index("fsdp")
    x, y, c = dp % 4, fs // 4, fs % 2
    h, j = (fs // 2) % 2, dp // 4
    z = h * 4 + j
    par = x % 2

    def dev(px, py, pz, pc=None):
        px, py, pz = (px + 4) % 4, (py + 4) % 4, (pz + 8) % 8
        return {"dp": (pz % 4) * 4 + px, "fsdp": (py * 2 + pz // 4) * 2 + (c if pc is None else pc)}

    sib = dev(x, y, z, 1 - c)
    xd = lambda d: dev(x + d, y, z)
    yd = lambda d: dev(x, y + d, z)
    zd = lambda d: dev(x, y, z + d)

    def copy(src, dst, sem, to):
        return pltpu.make_async_remote_copy(
            src_ref=src, dst_ref=dst, send_sem=ss.at[sem], recv_sem=rs.at[sem], device_id=to, device_id_type=MESH
        )

    hid_copy = pltpu.make_async_copy(hidden, hid, lsem.at[0])
    hid_copy.start()
    own = y * 2 + h
    head_copy = pltpu.make_async_copy(heads, pg.at[1, own], lsem.at[1])
    head_copy.start()

    barrier = pltpu.get_barrier_semaphore()
    everyone = [sib] + [xd(d) for d in (1, 2, 3)] + [yd(d) for d in (1, 2, 3)] + [zd(d) for d in range(1, 8)]
    for to in everyone:
        pl.semaphore_signal(barrier, inc=1, device_id=to, device_id_type=MESH)

    pg[0, own] = (weight[...].astype(f32) * scale[...].astype(f32)).astype(bf16)
    idb[pl.ds(c, 1)] = ids[...][None]
    pl.semaphore_wait(barrier, len(everyone))

    def slot(role):
        off = jnp.where(role % 4 == 1, 3, jnp.where(role % 4 == 2, 1, jnp.where(role % 4 == 3, 2, 0)))
        return ((y + off) % 4) * 2 + jnp.where(role < 4, h, 1 - h)

    def piece(m, role, start, count):
        return pg.at[m, slot(role), pl.ds(pl.multiple_of(start, 64), count)]

    q0, q1, rest = par * 128, par * 128 + 64, (1 - par) * 128
    o0, o1 = (1 - par) * 128, (1 - par) * 128 + 64

    def move(m, role, start, count, sem, to):
        ref = piece(m, role, start, count)
        return copy(ref, ref, m * GATHER + sem, to)

    def y_sends(m):
        for sem, plus, minus, count in ((Y_A, q0, q1, 64), (Y_B, q1, q0, 64), (Y_C, rest, rest, 128)):
            move(m, 0, plus, count, sem, yd(1)).start()
            move(m, 0, minus, count, sem + 1, yd(-1)).start()

    def z_source(m, k):
        @pl.when(j == 3)
        def _():
            move(m, k, q0, 64, ZU + k, zd(1)).start()

        @pl.when(j == 0)
        def _():
            move(m, k, q1, 64, ZD + k, zd(-1)).start()

    def y_quarters(m):
        move(m, 1, q0, 64, Y_A, yd(1)).wait_recv()
        move(m, 1, q0, 64, Y2, yd(1)).start()
        move(m, 2, q1, 64, Y_A + 1, yd(-1)).wait_recv()
        move(m, 2, q1, 64, Y2 + 1, yd(-1)).start()
        move(m, 1, q1, 64, Y_B, yd(1)).wait_recv()
        z_source(m, 1)
        move(m, 2, q0, 64, Y_B + 1, yd(-1)).wait_recv()
        z_source(m, 2)

    def y_rest(m):
        move(m, 1, rest, 128, Y_C, yd(1)).wait_recv()
        move(m, 2, rest, 128, Y_C + 1, yd(-1)).wait_recv()

    def x_up(m, role):
        move(m, role, q0, 64, XQ + 2 * (role - 3), xd(1)).start()

    def x_down(m, role):
        move(m, role, q1, 64, XQ + 2 * (role - 3) + 1, xd(-1)).start()

    def y_far(m):
        move(m, 3, q0, 64, Y2, yd(1)).wait_recv()
        x_up(m, 3)
        move(m, 3, q1, 64, Y2 + 1, yd(-1)).wait_recv()
        x_down(m, 3)
        z_source(m, 3)

    def z_step(n):
        up, down = n - 2 * j, n - 2 * (3 - j)

        @pl.when(jnp.logical_and(up >= 0, up < 8))
        def _():
            m, k = up // 4, up % 4
            move(m, 4 + k, q0, 64, ZU + k, zd(1)).wait_recv()

            @pl.when(j < 3)
            def _():
                move(m, 4 + k, q0, 64, ZU + k, zd(1)).start()

            x_up(m, 4 + k)

        @pl.when(jnp.logical_and(down >= 0, down < 8))
        def _():
            m, k = down // 4, down % 4
            move(m, 4 + k, q1, 64, ZD + k, zd(-1)).wait_recv()

            @pl.when(j > 0)
            def _():
                move(m, 4 + k, q1, 64, ZD + k, zd(-1)).start()

            x_down(m, 4 + k)

    def x_wait(m, role):
        sem = XQ + 2 * (role - 3)
        move(m, role, o0, 64, sem, xd(1)).wait_recv()
        move(m, role, o1, 64, sem + 1, xd(-1)).wait_recv()

    def to_sibling(role):
        s = slot(role)
        return copy(pg.at[0, s], ws.at[s], SIB_W + role, sib)

    def project(role):
        to_sibling(role).wait_recv()
        s = slot(role)

        @pl.loop(0, 4)
        def _(n):
            cols = pl.ds(pl.multiple_of(n * 256, 256), 256)
            acc[:, cols] += jnp.dot(normed[s, c], pg[0, s, :, cols], preferred_element_type=f32) + jnp.dot(
                normed[s, 1 - c], ws[s, :, cols], preferred_element_type=f32
            )

    y_sends(0)
    z_source(0, 0)
    to_sibling(0).start()
    id_copy = copy(idb.at[c], idb.at[c], SIB_I, sib)
    id_copy.start()
    hid_copy.wait()

    @pl.loop(0, 32)
    def _(r):
        at = pl.ds(pl.multiple_of(r * 16, 16), 16)
        block = hid[at, :].astype(f32)
        inv = lax.rsqrt(jnp.mean(block * block, axis=-1, keepdims=True) + eps)
        out = (block * inv * t_gain[...]).astype(bf16)
        for s in range(16):
            normed[s // 2, s % 2, at, :] = out[:, s * 256 : (s + 1) * 256]

    acc[...] = jnp.zeros_like(acc)
    head_copy.wait()
    z_step(0)
    y_quarters(0)
    y_sends(1)
    z_source(1, 0)
    z_step(1)
    z_step(2)
    y_far(0)
    z_step(3)
    y_quarters(1)
    z_step(4)
    z_step(5)
    y_far(1)
    y_rest(0)
    to_sibling(1).start()
    to_sibling(2).start()
    project(0)
    z_step(6)
    project(1)
    z_step(7)
    project(2)
    x_wait(0, 3)
    to_sibling(3).start()
    z_step(8)
    project(3)
    x_wait(0, 4)
    to_sibling(4).start()
    z_step(9)
    project(4)
    x_wait(0, 5)
    to_sibling(5).start()
    z_step(10)
    project(5)
    x_wait(0, 6)
    to_sibling(6).start()
    z_step(11)
    project(6)
    x_wait(0, 7)
    to_sibling(7).start()
    z_step(12)
    project(7)

    @pl.loop(0, 16)
    def _(r):
        at = pl.ds(pl.multiple_of(r * 32, 32), 32)
        block = acc[at, :]
        inv = lax.rsqrt(jnp.mean(block * block, axis=-1, keepdims=True) + eps)
        rows[pl.ds(pl.multiple_of(c * 512 + r * 32, 32), 32), :] = (block * inv * d_gain[...]).astype(bf16)

    my_rows = rows.at[pl.ds(pl.multiple_of(c * 512, 512), 512)]
    row_copy = copy(my_rows, my_rows, SIB_R, sib)
    sums[...] = jnp.zeros_like(sums)
    row_copy.start()
    z_step(13)
    id_copy.wait_recv()
    row_copy.wait_recv()
    y_rest(1)

    def score(role):
        s = slot(role)

        @pl.loop(0, 4)
        def _(n):
            cols = pl.ds(pl.multiple_of(n * 256, 256), 256)
            got = lax.dot_general(
                pg[1, s], rows[cols, :], (((1,), (1,)), ((), ())), preferred_element_type=f32
            )
            t = jnp.tanh(got * (1.0 / cap))
            e = jnp.exp(t * cap)
            tb[s, :, cols] = t
            eb[s, :, cols] = e
            ids_at = idb[n // 2, :, pl.ds(pl.multiple_of((n % 2) * 256, 256), 256)]
            card = lax.broadcasted_iota(jnp.int32, (64, 256), 0) + (s * 2 + c) * 64
            for k in range(4):
                part = slice(k * 64, (k + 1) * 64)
                hit = card == ids_at[k : k + 1, :]
                sums[c, k : k + 1, cols] += jnp.sum(e[part], axis=0, keepdims=True)
                sums[c, k + 4 : k + 5, cols] += jnp.sum(jnp.where(hit, t[part], 0.0), axis=0, keepdims=True)

    @pl.loop(0, 3)
    def _(role):
        score(role)

    @pl.loop(3, 8)
    def _(role):
        x_wait(1, role)
        score(role)

    my_sums = sums.at[c]
    sum_copy = copy(my_sums, my_sums, SIB_S, sib)
    sum_copy.start()
    sum_copy.wait_recv()
    totals = sums[0, 0:4, :] + sums[1, 0:4, :]
    mine_f = pl.ds(pl.multiple_of(c * 512, 512), 512)
    loss_out[...] = jnp.log(sums[0, 0:4, mine_f] + sums[1, 0:4, mine_f]) - cap * (
        sums[0, 4:8, mine_f] + sums[1, 4:8, mine_f]
    )
    sum_copy.wait_send()
    sums[c, 0:4, :] = 1.0 / totals

    def gradient(i):
        hp = i % 2
        s = 1 - 2 * hp
        step = i // 2
        off = jnp.where(step == 0, 2, jnp.where(step == 1, 4 - s, jnp.where(step == 2, 4 + s, 0)))
        b = ((y + off) % 4) * 2 + hp

        @pl.loop(0, 4)
        def _(n):
            cols = pl.ds(pl.multiple_of(n * 256, 256), 256)
            ids_at = idb[n // 2, :, pl.ds(pl.multiple_of((n % 2) * 256, 256), 256)]
            card = lax.broadcasted_iota(jnp.int32, (64, 256), 0) + (b * 2 + c) * 64
            for k in range(4):
                part = slice(k * 64, (k + 1) * 64)
                t = tb[b, part, cols]
                p = eb[b, part, cols] * sums[c, k : k + 1, cols]
                hit = card == ids_at[k : k + 1, :]
                p = jnp.where(hit, p - 1.0, p)
                dl[part, cols] = (p * ((1.0 - t * t) * loss_scale)).astype(bf16)

        @pl.loop(0, 4)
        def _(n):
            cols = pl.ds(pl.multiple_of(n * 256, 256), 256)
            g = jnp.dot(dl[...], rows[:, cols], preferred_element_type=f32)
            eb[b, :, cols] = g
            gb[b, :, cols] = g.astype(bf16)

        head = lambda d: pl.ds(pl.multiple_of(((x + d + 4) % 4) * 64, 64), 64)
        copy(gb.at[b, head(2), pl.ds(0, 512)], ra2.at[b], A2 + b, xd(s)).start()
        copy(gb.at[b, head(-s), pl.ds(0, 512)], ra1m.at[b], A1M + b, xd(-s)).start()

        @pl.when(step == 0)
        def _():
            copy(gb.at[b, :, pl.ds(512, 512)], rb2.at[hp], B2 + hp, yd(s)).start()

        @pl.when(step == 1)
        def _():
            copy(gb.at[b, :, pl.ds(512, 512)], rb1m.at[hp], B1M + hp, yd(-s)).start()

    @pl.loop(0, 8)
    def _(i):
        gradient(i)

    for hp in range(2):
        s = 1 - 2 * hp
        b = ((y + s + 4) % 4) * 2 + hp
        copy(sab.at[hp], rb2.at[hp], B2 + hp, yd(s)).wait_recv()
        for r in range(4):
            part = slice(r * 64, (r + 1) * 64)
            sab[hp, part, :] = (eb[b, part, 512:1024] + rb2[hp, part, :].astype(f32)).astype(bf16)
        copy(sab.at[hp], rb1a.at[hp], B1A + hp, yd(s)).start()

    @pl.loop(0, 8)
    def _(b):
        s = 1 - 2 * (b % 2)
        at = pl.ds(pl.multiple_of(((x + s + 4) % 4) * 64, 64), 64)
        copy(saa.at[b], ra2.at[b], A2 + b, xd(s)).wait_recv()
        saa[b] = (eb[b, at, 0:512] + ra2[b].astype(f32)).astype(bf16)
        copy(saa.at[b], ra1a.at[b], A1A + b, xd(s)).start()

    my_head = pl.ds(pl.multiple_of(x * 64, 64), 64)
    for hp in range(2):
        s = 1 - 2 * hp
        copy(sab.at[hp], rb1m.at[hp], B1M + hp, yd(-s)).wait_recv()
        copy(sab.at[hp], rb1a.at[hp], B1A + hp, yd(s)).wait_recv()
        for r in range(4):
            part = slice(r * 64, (r + 1) * 64)
            sb[hp, part, :] = (
                eb[y * 2 + hp, part, 512:1024] + rb1m[hp, part, :].astype(f32) + rb1a[hp, part, :].astype(f32)
            )
    for d in (2, 1, 3):
        at = pl.ds(pl.multiple_of(((x + d) % 4) * 64, 64), 64)
        s2b[d - 1] = sb[:, at, :].astype(bf16)
        copy(s2b.at[d - 1], r2b.at[d - 1], S2B + d - 1, xd(d)).start()

    @pl.loop(0, 8)
    def _(b):
        s = 1 - 2 * (b % 2)
        copy(saa.at[b], ra1m.at[b], A1M + b, xd(-s)).wait_recv()
        copy(saa.at[b], ra1a.at[b], A1A + b, xd(s)).wait_recv()
        sa[b] = eb[b, my_head, 0:512] + ra1m[b].astype(f32) + ra1a[b].astype(f32)

    for d in (2, 1, 3):
        s2a[d - 1] = sa[pl.ds(((y + d) % 4) * 2, 2)].astype(bf16)
        copy(s2a.at[d - 1], r2a.at[d - 1], S2A + d - 1, yd(d)).start()

    for d in range(3):
        copy(s2b.at[d], r2b.at[d], S2B + d, xd(d + 1)).wait_recv()
    tt[:, :, 512:1024] = (
        sb[:, my_head, :] + r2b[0].astype(f32) + r2b[1].astype(f32) + r2b[2].astype(f32)
    )
    for d in range(3):
        copy(s2a.at[d], r2a.at[d], S2A + d, yd(d + 1)).wait_recv()
    tt[:, :, 0:512] = (
        sa[pl.ds(y * 2, 2)] + r2a[0].astype(f32) + r2a[1].astype(f32) + r2a[2].astype(f32)
    )
    s3[...] = tt[...].astype(bf16)
    for d in (4, 3, 5, 2, 6, 1, 7):
        to = (z + d) % 8
        at = pl.ds(pl.multiple_of((to % 4) * 16, 16), 16)
        copy(s3.at[to // 4, at], r3.at[d - 1], S3 + d - 1, zd(d)).start()
    strip = pl.ds(pl.multiple_of(j * 16, 16), 16)
    total = tt[h, strip, :]
    for d in (1, 7, 2, 6, 3, 5, 4):
        copy(r3.at[d - 1], r3.at[d - 1], S3 + d - 1, zd(d)).wait_recv()
        total = total + r3[d - 1].astype(f32)

    fin[x, strip, :] = total.astype(bf16)
    def z_share(d):
        to = h * 4 + (j + d) % 4
        return copy(fin.at[x, strip], fin.at[x, strip], GZ + d - 1, dev(x, y, to))
    for d in (2, 1, 3):
        z_share(d).start()
    for d in (1, 2, 3):
        z_share(d).wait_recv()
    def x_share(d):
        return copy(fin.at[x], fin.at[x], GX + d - 1, xd(d))
    for d in (2, 1, 3):
        x_share(d).start()
    grad_out[x] = fin[x].astype(f32)
    for d in (1, 3, 2):
        x_share(d).wait_recv()
        src = (x + 4 - d) % 4
        grad_out[src] = fin[src].astype(f32)

    for m in range(2):
        for sem, count in ((Y_A, 64), (Y_A + 1, 64), (Y_B, 64), (Y_B + 1, 64), (Y_C, 128), (Y_C + 1, 128)):
            move(m, 0, 0, count, sem, yd(1)).wait_send()
        for sem in range(Y2, GATHER):
            move(m, 0, 0, 64, sem, yd(1)).wait_send()
    for role in range(8):
        to_sibling(role).wait_send()
    row_copy.wait_send()
    id_copy.wait_send()
    for b in range(8):
        for sem in (A2, A1M, A1A):
            copy(saa.at[b], ra2.at[b], sem + b, sib).wait_send()
    for hp in range(2):
        for sem in (B2, B1M, B1A):
            copy(sab.at[hp], rb2.at[hp], sem + hp, sib).wait_send()
    for d in range(3):
        copy(s2a.at[d], r2a.at[d], S2A + d, sib).wait_send()
        copy(s2b.at[d], r2b.at[d], S2B + d, sib).wait_send()
        z_share(d + 1).wait_send()
        x_share(d + 1).wait_send()
    for d in range(7):
        copy(r3.at[d], r3.at[d], S3 + d, sib).wait_send()


def shards(hidden, temporal_gain, in_weight, in_scale, depth_gain, head_weight, code_ids):
    vmem = pl.BlockSpec(memory_space=pltpu.VMEM)
    hbm = pl.BlockSpec(memory_space=pl.ANY)
    V = pltpu.VMEM
    loss, grad = pl.pallas_call(
        kernel,
        out_shape=(jax.ShapeDtypeStruct((4, 512), f32), jax.ShapeDtypeStruct((4, 64, 1024), f32)),
        in_specs=[hbm, vmem, vmem, vmem, vmem, hbm, vmem],
        out_specs=(vmem, vmem),
        scratch_shapes=[
            V((512, 4096), bf16), V((8, 2, 512, 256), bf16), V((2, 8, 256, 1024), bf16), V((8, 256, 1024), bf16),
            V((512, 1024), f32), V((1024, 1024), bf16), V((8, 256, 1024), f32), V((8, 256, 1024), f32),
            V((256, 1024), bf16), V((8, 256, 1024), bf16),
            V((8, 64, 512), bf16), V((8, 64, 512), bf16), V((8, 64, 512), bf16), V((8, 64, 512), bf16),
            V((2, 256, 512), bf16), V((2, 256, 512), bf16), V((2, 256, 512), bf16), V((2, 256, 512), bf16),
            V((8, 64, 512), f32), V((2, 256, 512), f32),
            V((3, 2, 64, 512), bf16), V((3, 2, 64, 512), bf16), V((3, 2, 64, 512), bf16), V((3, 2, 64, 512), bf16),
            V((2, 64, 1024), f32), V((2, 64, 1024), bf16), V((7, 16, 1024), bf16), V((4, 64, 1024), bf16),
            V((2, 4, 512), jnp.int32), V((2, 8, 1024), f32),
            pltpu.SemaphoreType.DMA((2,)), pltpu.SemaphoreType.DMA((N_SEM,)), pltpu.SemaphoreType.DMA((N_SEM,)),
        ],
        compiler_params=pltpu.CompilerParams(
            collective_id=0, has_side_effects=True, vmem_limit_bytes=63 * 2**20
        ),
    )(
        hidden, temporal_gain[None, :], in_weight, in_scale[:, None], depth_gain[None, :],
        head_weight.reshape(256, 1024), code_ids.T,
    )
    return loss.T, grad


def solution(mesh):
    in_specs = (
        P(("dp", "fsdp"), None),
        P(),
        P("fsdp", None),
        P("fsdp"),
        P(),
        P(None, "fsdp", None),
        P(("dp", "fsdp"), None),
    )
    out_specs = (P(("dp", "fsdp"), None), P(None, "fsdp", None))
    return jax.shard_map(shards, mesh=mesh, in_specs=in_specs, out_specs=out_specs, check_vma=False)
```

```python
import functools

import jax
import jax.numpy as jnp
from jax import lax
from jax.experimental import pallas as pl
from jax.experimental.pallas import tpu as pltpu
from jax.sharding import PartitionSpec as P

MESH = pl.DeviceIdType.MESH
f32, bf16 = jnp.float32, jnp.bfloat16
eps = 1e-05
cap = 30.0
loss_scale = 0.0625

Y_A, Y_B, Y_C, Y2, ZU, ZD, XQ = 0, 2, 4, 6, 8, 16, 24
GATHER = 44
SIB_W, SIB_R, SIB_S, SIB_I = 88, 96, 97, 98
RS = 99
A2, A1M, A1A, B2, B1M, B1A, S2A, S2B, S3, GZ, GX = 0, 8, 16, 24, 26, 28, 30, 33, 36, 43, 46
SUM = 58
N_SEM = RS + 2 * SUM
WIDTH = (384, 128)
A_COL = (0, WIDTH[0])
B_COL = (1024 - WIDTH[0], WIDTH[0] + WIDTH[1])


def kernel(
    hidden, t_gain, weight, scale, d_gain, heads, ids,
    loss_out, grad_out,
    hid, normed, pg, ws, acc, rows, tb, eb, dl, idb, sums, lsem, ss, rs, *parts,
):
    half_parts = len(parts) // 2
    parts = (parts[:half_parts], parts[half_parts:])
    dp, fs = lax.axis_index("dp"), lax.axis_index("fsdp")
    x, y, c = dp % 4, fs // 4, fs % 2
    h, j = (fs // 2) % 2, dp // 4
    z = h * 4 + j
    par = x % 2

    def dev(px, py, pz, pc=None):
        px, py, pz = (px + 4) % 4, (py + 4) % 4, (pz + 8) % 8
        return {"dp": (pz % 4) * 4 + px, "fsdp": (py * 2 + pz // 4) * 2 + (c if pc is None else pc)}

    sib = dev(x, y, z, 1 - c)
    xd = lambda d: dev(x + d, y, z)
    yd = lambda d: dev(x, y + d, z)
    zd = lambda d: dev(x, y, z + d)

    def copy(src, dst, sem, to):
        return pltpu.make_async_remote_copy(
            src_ref=src, dst_ref=dst, send_sem=ss.at[sem], recv_sem=rs.at[sem], device_id=to, device_id_type=MESH
        )

    hid_copy = pltpu.make_async_copy(hidden, hid, lsem.at[0])
    hid_copy.start()
    own = y * 2 + h
    head_copy = pltpu.make_async_copy(heads, pg.at[1, own], lsem.at[1])
    head_copy.start()

    barrier = pltpu.get_barrier_semaphore()
    everyone = [sib] + [xd(d) for d in (1, 2, 3)] + [yd(d) for d in (1, 2, 3)] + [zd(d) for d in range(1, 8)]
    for to in everyone:
        pl.semaphore_signal(barrier, inc=1, device_id=to, device_id_type=MESH)

    on_diagonal = lax.broadcasted_iota(jnp.int32, (256, 256), 0) == lax.broadcasted_iota(jnp.int32, (256, 256), 1)
    diagonal = jnp.where(on_diagonal, scale[...].astype(f32)[None, :], 0.0).astype(bf16)
    pg[0, own] = jnp.dot(diagonal, weight[...], preferred_element_type=f32).astype(bf16)
    idb[pl.ds(c, 1)] = ids[...][None]
    pl.semaphore_wait(barrier, len(everyone))

    def slot(role):
        off = jnp.where(role % 4 == 1, 3, jnp.where(role % 4 == 2, 1, jnp.where(role % 4 == 3, 2, 0)))
        return ((y + off) % 4) * 2 + jnp.where(role < 4, h, 1 - h)

    def piece(m, role, start, count):
        return pg.at[m, slot(role), pl.ds(pl.multiple_of(start, 32), count)]

    q0, q1, rest = par * 128, par * 128 + 64, (1 - par) * 128
    o0, o1 = (1 - par) * 128, (1 - par) * 128 + 64

    def move(m, role, start, count, sem, to):
        ref = piece(m, role, start, count)
        return copy(ref, ref, m * GATHER + sem, to)

    def y_send(m, sem):
        plus, minus, count = {Y_A: (q0, q1, 64), Y_B: (q1, q0, 64), Y_C: (rest, rest, 128)}[sem]
        move(m, 0, plus, count, sem, yd(1)).start()
        move(m, 0, minus, count, sem + 1, yd(-1)).start()

    def z_up(m, k, half):
        return move(m, k, q0 + 32 * half, 32, ZU + 2 * (k % 4) + half, zd(1))

    def z_down(m, k, half):
        return move(m, k, q1 + 32 * half, 32, ZD + 2 * (k % 4) + half, zd(-1))

    def y_sent(m, sem):
        move(m, 0, 0, 64, sem, yd(1)).wait_send()
        move(m, 0, 0, 64, sem + 1, yd(-1)).wait_send()

    def up_source(m, k):
        @pl.when(j == 3)
        def _():
            z_up(m, k, 0).start()
            z_up(m, k, 1).start()

    def down_source(m, k):
        @pl.when(j == 0)
        def _():
            z_down(m, k, 0).start()
            z_down(m, k, 1).start()

    def x_up(m, role, half):
        return move(m, role, q0 + 32 * half, 32, XQ + 4 * (role - 3) + 2 * half, xd(1))

    def x_down(m, role, half):
        return move(m, role, q1 + 32 * half, 32, XQ + 4 * (role - 3) + 2 * half + 1, xd(-1))

    def y_first(m):
        move(m, 1, q0, 64, Y_A, yd(1)).wait_recv()
        move(m, 1, q0, 64, Y2, yd(1)).start()
        up_source(m, 1)
        move(m, 2, q1, 64, Y_A + 1, yd(-1)).wait_recv()
        move(m, 2, q1, 64, Y2 + 1, yd(-1)).start()
        down_source(m, 2)

    def y_second(m):
        move(m, 1, q1, 64, Y_B, yd(1)).wait_recv()
        down_source(m, 1)
        move(m, 2, q0, 64, Y_B + 1, yd(-1)).wait_recv()
        up_source(m, 2)

    def y_rest(m):
        move(m, 1, rest, 128, Y_C, yd(1)).wait_recv()
        move(m, 2, rest, 128, Y_C + 1, yd(-1)).wait_recv()

    def y_far(m):
        move(m, 3, q0, 64, Y2, yd(1)).wait_recv()
        up_source(m, 3)
        x_up(m, 3, 0).start()
        x_up(m, 3, 1).start()
        move(m, 3, q1, 64, Y2 + 1, yd(-1)).wait_recv()
        down_source(m, 3)
        x_down(m, 3, 0).start()
        x_down(m, 3, 1).start()

    def z_piece(i, first):
        q = i // 2
        k = jnp.where(q < 2, 0, jnp.where(q < 5, q - 1, q - 4))
        k = jnp.where(k == 1, first, jnp.where(k == 2, 3 - first, k))
        return jnp.where(jnp.logical_or(q == 1, q >= 5), 1, 0), 4 + k, i % 2

    def z_step(n):
        up, down = n - 3 * j, n - 3 * (3 - j)

        @pl.when(jnp.logical_and(up >= 0, up < 16))
        def _():
            m, role, half = z_piece(up, 1)
            z_up(m, role, half).wait_recv()

            @pl.when(j < 3)
            def _():
                z_up(m, role, half).start()

            x_up(m, role, half).start()

        @pl.when(jnp.logical_and(down >= 0, down < 16))
        def _():
            m, role, half = z_piece(down, 2)
            z_down(m, role, half).wait_recv()

            @pl.when(j > 0)
            def _():
                z_down(m, role, half).start()

            x_down(m, role, half).start()

    def x_wait(m, role):
        for half in range(2):
            sem = XQ + 4 * (role - 3) + 2 * half
            move(m, role, o0 + 32 * half, 32, sem, xd(1)).wait_recv()
            move(m, role, o1 + 32 * half, 32, sem + 1, xd(-1)).wait_recv()

    def to_sibling(role):
        s = slot(role)
        return copy(pg.at[0, s], ws.at[s], SIB_W + role, sib)

    def project(role):
        to_sibling(role).wait_recv()
        s = slot(role)

        @pl.loop(0, 4)
        def _(n):
            cols = pl.ds(pl.multiple_of(n * 256, 256), 256)
            acc[:, cols] += jnp.dot(normed[s, c], pg[0, s, :, cols], preferred_element_type=f32) + jnp.dot(
                normed[s, 1 - c], ws[s, :, cols], preferred_element_type=f32
            )

    y_send(0, Y_A)
    up_source(0, 0)
    down_source(0, 0)
    to_sibling(0).start()
    id_copy = copy(idb.at[c], idb.at[c], SIB_I, sib)
    id_copy.start()
    head_copy.wait()
    up_source(1, 0)
    down_source(1, 0)
    acc[...] = jnp.zeros_like(acc)
    sums[...] = jnp.zeros_like(sums)
    hid_copy.wait()

    def norm(part):
        @pl.loop(part * 4, part * 4 + 4)
        def _(r):
            at = pl.ds(pl.multiple_of(r * 16, 16), 16)
            block = hid[at, :].astype(f32)
            inv = lax.rsqrt(jnp.mean(block * block, axis=-1, keepdims=True) + eps)
            out = (block * inv * t_gain[...]).astype(bf16)
            for s in range(16):
                normed[s // 2, s % 2, at, :] = out[:, s * 256 : (s + 1) * 256]

    norm(0)
    norm(1)
    y_sent(0, Y_A)
    y_send(0, Y_B)
    z_step(0)
    y_first(0)
    z_step(1)
    norm(2)
    z_step(2)
    y_sent(0, Y_B)
    y_send(1, Y_A)
    z_step(3)
    y_second(0)
    z_step(4)
    norm(3)
    z_step(5)
    y_far(0)
    y_sent(1, Y_A)
    y_send(1, Y_B)
    z_step(6)
    y_first(1)
    norm(4)
    z_step(7)
    y_sent(1, Y_B)
    y_send(0, Y_C)
    z_step(8)
    y_second(1)
    norm(5)
    z_step(9)
    z_step(10)
    y_far(1)
    norm(6)
    z_step(11)
    norm(7)
    z_step(12)
    y_rest(0)
    to_sibling(1).start()
    to_sibling(2).start()
    y_send(1, Y_C)
    z_step(13)
    x_wait(0, 3)
    to_sibling(3).start()
    project(0)
    z_step(14)
    x_wait(0, 4)
    to_sibling(4).start()
    project(1)
    z_step(15)
    project(2)
    z_step(16)
    project(3)
    z_step(17)
    project(4)
    z_step(18)
    z_step(19)
    x_wait(0, 5)
    to_sibling(5).start()
    x_wait(0, 6)
    to_sibling(6).start()
    z_step(20)
    project(5)
    z_step(21)
    project(6)
    x_wait(0, 7)
    to_sibling(7).start()
    z_step(22)
    project(7)

    @pl.loop(0, 16)
    def _(r):
        at = pl.ds(pl.multiple_of(r * 32, 32), 32)
        block = acc[at, :]
        inv = lax.rsqrt(jnp.mean(block * block, axis=-1, keepdims=True) + eps)
        rows[pl.ds(pl.multiple_of(c * 512 + r * 32, 32), 32), :] = (block * inv * d_gain[...]).astype(bf16)

    my_rows = rows.at[pl.ds(pl.multiple_of(c * 512, 512), 512)]
    row_copy = copy(my_rows, my_rows, SIB_R, sib)
    row_copy.start()
    z_step(23)
    z_step(24)
    id_copy.wait_recv()
    y_rest(1)
    for role in range(3, 8):
        x_wait(1, role)

    def score(n):
        cols = pl.ds(pl.multiple_of(n * 256, 256), 256)
        got = lax.dot_general(
            pg[1].reshape(2048, 1024), rows[cols, :], (((1,), (1,)), ((), ())), preferred_element_type=f32
        )
        tb[:, :, cols] = got.reshape(8, 256, 256)
        ids_at = idb[n // 2, :, pl.ds(pl.multiple_of((n % 2) * 256, 256), 256)]

        @pl.loop(0, 8)
        def _(b):
            card = lax.broadcasted_iota(jnp.int32, (64, 256), 0) + (b * 2 + c) * 64
            for k in range(4):
                part = slice(k * 64, (k + 1) * 64)
                t = jnp.tanh(tb[b, part, cols] * (1.0 / cap))
                e = jnp.exp(t * cap)
                tb[b, part, cols] = t
                eb[b, part, cols] = e
                hit = card == ids_at[k : k + 1, :]
                sums[c, k : k + 1, cols] += jnp.sum(e, axis=0, keepdims=True)
                sums[c, k + 4 : k + 5, cols] += jnp.sum(jnp.where(hit, t, 0.0), axis=0, keepdims=True)

    @pl.loop(0, 2)
    def _(n):
        score(c * 2 + n)

    row_copy.wait_recv()

    @pl.loop(0, 2)
    def _(n):
        score((1 - c) * 2 + n)

    my_sums = sums.at[c]
    sum_copy = copy(my_sums, my_sums, SIB_S, sib)
    sum_copy.start()
    sum_copy.wait_recv()
    totals = sums[0, 0:4, :] + sums[1, 0:4, :]
    mine_f = pl.ds(pl.multiple_of(c * 512, 512), 512)
    loss_out[...] = jnp.log(sums[0, 0:4, mine_f] + sums[1, 0:4, mine_f]) - cap * (
        sums[0, 4:8, mine_f] + sums[1, 4:8, mine_f]
    )
    sum_copy.wait_send()
    sums[c, 0:4, :] = 1.0 / totals

    def logits(b):
        @pl.loop(0, 4)
        def _(n):
            cols = pl.ds(pl.multiple_of(n * 256, 256), 256)
            ids_at = idb[n // 2, :, pl.ds(pl.multiple_of((n % 2) * 256, 256), 256)]
            card = lax.broadcasted_iota(jnp.int32, (64, 256), 0) + (b * 2 + c) * 64
            for k in range(4):
                part = slice(k * 64, (k + 1) * 64)
                t = tb[b, part, cols]
                p = eb[b, part, cols] * sums[c, k : k + 1, cols]
                hit = card == ids_at[k : k + 1, :]
                p = jnp.where(hit, p - 1.0, p)
                dl[b, part, cols] = (p * ((1.0 - t * t) * loss_scale)).astype(bf16)

    head = lambda d: pl.ds(pl.multiple_of(((x + d + 4) % 4) * 64, 64), 64)
    my_head = head(0)
    strip = pl.ds(pl.multiple_of(j * 16, 16), 16)

    class Part:
        def __init__(self, q):
            self.w, self.a, self.b, self.base = WIDTH[q], A_COL[q], B_COL[q], RS + q * SUM
            (self.ga, self.gb, self.ra2, self.ra1m, self.ra1a, self.saa, self.rb2, self.rb1m, self.rb1a, self.sab,
             self.sa, self.sb, self.s2a, self.r2a, self.s2b, self.r2b, self.tt, self.s3, self.r3, self.fin) = parts[q]

        def send(self, src, dst, sem, to):
            return copy(src, dst, self.base + sem, to)

        def gradient(self, i):
            b0 = ((y + jnp.where(i == 0, 2, jnp.where(i == 1, 1, jnp.where(i == 2, 3, 0)))) % 4) * 2
            if self.base == RS:
                logits(b0)
                logits(b0 + 1)
            both = pl.ds(b0, 2)
            for col, out in ((self.a, self.ga), (self.b, self.gb)):
                g = jnp.dot(
                    dl[both].reshape(512, 1024), rows[:, col : col + self.w], preferred_element_type=f32
                ).reshape(2, 256, self.w)
                eb[both, :, col : col + self.w] = g
                out[both] = g.astype(bf16)
            for hp in range(2):
                s, b = 1 - 2 * hp, b0 + hp
                self.send(self.ga.at[b, head(2)], self.ra2.at[b], A2 + b, xd(s)).start()
                self.send(self.ga.at[b, head(-s)], self.ra1m.at[b], A1M + b, xd(-s)).start()

                @pl.when(i == 0)
                def _():
                    self.send(self.gb.at[b], self.rb2.at[hp], B2 + hp, yd(s)).start()

                @pl.when(i == 2 - hp)
                def _():
                    self.send(self.gb.at[b], self.rb1m.at[hp], B1M + hp, yd(-s)).start()

        def ride(self):
            for hp in range(2):
                s = 1 - 2 * hp
                b = ((y + s + 4) % 4) * 2 + hp
                self.send(self.sab.at[hp], self.rb2.at[hp], B2 + hp, yd(s)).wait_recv()
                for r in range(4):
                    at = slice(r * 64, (r + 1) * 64)
                    self.sab[hp, at, :] = (
                        eb[b, at, self.b : self.b + self.w] + self.rb2[hp, at, :].astype(f32)
                    ).astype(bf16)
                self.send(self.sab.at[hp], self.rb1a.at[hp], B1A + hp, yd(s)).start()

            @pl.loop(0, 8)
            def _(b):
                s = 1 - 2 * (b % 2)
                self.send(self.saa.at[b], self.ra2.at[b], A2 + b, xd(s)).wait_recv()
                self.saa[b] = (eb[b, head(s), self.a : self.a + self.w] + self.ra2[b].astype(f32)).astype(bf16)
                self.send(self.saa.at[b], self.ra1a.at[b], A1A + b, xd(s)).start()

        def first(self):
            for hp in range(2):
                s = 1 - 2 * hp
                self.send(self.sab.at[hp], self.rb1m.at[hp], B1M + hp, yd(-s)).wait_recv()
                self.send(self.sab.at[hp], self.rb1a.at[hp], B1A + hp, yd(s)).wait_recv()
                for r in range(4):
                    at = slice(r * 64, (r + 1) * 64)
                    self.sb[hp, at, :] = (
                        eb[y * 2 + hp, at, self.b : self.b + self.w]
                        + self.rb1m[hp, at, :].astype(f32)
                        + self.rb1a[hp, at, :].astype(f32)
                    )
            for d in (2, 1, 3):
                self.s2b[d - 1] = self.sb[:, head(d), :].astype(bf16)
                self.send(self.s2b.at[d - 1], self.r2b.at[d - 1], S2B + d - 1, xd(d)).start()

            @pl.loop(0, 8)
            def _(b):
                s = 1 - 2 * (b % 2)
                self.send(self.saa.at[b], self.ra1m.at[b], A1M + b, xd(-s)).wait_recv()
                self.send(self.saa.at[b], self.ra1a.at[b], A1A + b, xd(s)).wait_recv()
                self.sa[b] = (
                    eb[b, my_head, self.a : self.a + self.w] + self.ra1m[b].astype(f32) + self.ra1a[b].astype(f32)
                )

            for d in (2, 1, 3):
                self.s2a[d - 1] = self.sa[pl.ds(((y + d) % 4) * 2, 2)].astype(bf16)
                self.send(self.s2a.at[d - 1], self.r2a.at[d - 1], S2A + d - 1, yd(d)).start()

        def second(self):
            w = self.w
            for d in range(3):
                self.send(self.s2b.at[d], self.r2b.at[d], S2B + d, xd(d + 1)).wait_recv()
            self.tt[:, :, w:] = (
                self.sb[:, my_head, :]
                + self.r2b[0].astype(f32) + self.r2b[1].astype(f32) + self.r2b[2].astype(f32)
            )
            for d in range(3):
                self.send(self.s2a.at[d], self.r2a.at[d], S2A + d, yd(d + 1)).wait_recv()
            self.tt[:, :, :w] = (
                self.sa[pl.ds(y * 2, 2)]
                + self.r2a[0].astype(f32) + self.r2a[1].astype(f32) + self.r2a[2].astype(f32)
            )
            self.s3[...] = self.tt[...].astype(bf16)
            for d in (4, 3, 5, 2, 6, 1, 7):
                to = (z + d) % 8
                at = pl.ds(pl.multiple_of((to % 4) * 16, 16), 16)
                self.send(self.s3.at[to // 4, at], self.r3.at[d - 1], S3 + d - 1, zd(d)).start()

        def z_share(self, d):
            here = self.fin.at[x, strip]
            return self.send(here, here, GZ + d - 1, dev(x, y, h * 4 + (j + d) % 4))

        def x_share(self, e, d):
            here = self.fin.at[x, pl.ds(pl.multiple_of(((j + 4 - e) % 4) * 16, 16), 16)]
            return self.send(here, here, GX + 3 * e + d - 1, xd(d))

        def third(self):
            total = self.tt[h, strip, :]
            for d in (1, 7, 2, 6, 3, 5, 4):
                self.send(self.r3.at[d - 1], self.r3.at[d - 1], S3 + d - 1, zd(d)).wait_recv()
                total = total + self.r3[d - 1].astype(f32)
            self.fin[x, strip, :] = total.astype(bf16)
            for d in (2, 1, 3):
                self.z_share(d).start()
            for d in (2, 1, 3):
                self.x_share(0, d).start()

        def share(self):
            for e in (1, 3, 2):
                self.z_share(e).wait_recv()
                for d in (2, 1, 3):
                    self.x_share(e, d).start()
            self.store(x)

        def store(self, k):
            grad_out[k, :, self.a : self.a + self.w] = self.fin[k, :, : self.w]
            grad_out[k, :, self.b : self.b + self.w] = self.fin[k, :, self.w :]

        def finish(self):
            for d in (1, 3, 2):
                for e in (0, 1, 3, 2):
                    self.x_share(e, d).wait_recv()
                self.store((x + 4 - d) % 4)

        def sent(self):
            for b in range(8):
                for sem in (A2, A1M, A1A):
                    self.send(self.saa.at[b], self.ra2.at[b], sem + b, sib).wait_send()
            for hp in range(2):
                for sem in (B2, B1M, B1A):
                    self.send(self.sab.at[hp], self.rb2.at[hp], sem + hp, sib).wait_send()
            for d in range(3):
                self.send(self.s2a.at[d], self.r2a.at[d], S2A + d, sib).wait_send()
                self.send(self.s2b.at[d], self.r2b.at[d], S2B + d, sib).wait_send()
                self.z_share(d + 1).wait_send()
                for e in range(4):
                    self.x_share(e, d + 1).wait_send()
            for d in range(7):
                self.send(self.r3.at[d], self.r3.at[d], S3 + d, sib).wait_send()

    one, two = Part(0), Part(1)

    @pl.loop(0, 4)
    def _(i):
        one.gradient(i)

    @pl.loop(0, 4)
    def _(i):
        two.gradient(i)

    one.ride()
    two.ride()
    one.first()
    one.second()
    two.first()
    one.third()
    two.second()
    one.share()
    two.third()
    two.share()
    one.finish()
    two.finish()

    for m in range(2):
        for sem, count in ((Y_C, 128), (Y_C + 1, 128)):
            move(m, 0, 0, count, sem, yd(1)).wait_send()
        for sem in (Y2, Y2 + 1):
            move(m, 0, 0, 64, sem, yd(1)).wait_send()
        for sem in range(ZU, GATHER):
            move(m, 0, 0, 32, sem, yd(1)).wait_send()
    for role in range(8):
        to_sibling(role).wait_send()
    row_copy.wait_send()
    id_copy.wait_send()
    one.sent()
    two.sent()


def widen(loss, grad, loss_out, grad_out):
    loss_out[...] = loss[...]
    grad_out[...] = grad[...].astype(f32)


def part_scratch(w):
    shapes = (
        [((8, 256, w), bf16)] * 2 + [((8, 64, w), bf16)] * 4 + [((2, 256, w), bf16)] * 4
        + [((8, 64, w), f32), ((2, 256, w), f32)] + [((3, 2, 64, w), bf16)] * 4
        + [((2, 64, 2 * w), f32), ((2, 64, 2 * w), bf16), ((7, 16, 2 * w), bf16), ((4, 64, 2 * w), bf16)]
    )
    return [pltpu.VMEM(shape, kind) for shape, kind in shapes]


def shards(hidden, temporal_gain, in_weight, in_scale, depth_gain, head_weight, code_ids):
    vmem = pl.BlockSpec(memory_space=pltpu.VMEM)
    hbm = pl.BlockSpec(memory_space=pl.ANY)
    V = pltpu.VMEM
    loss, grad = pl.pallas_call(
        kernel,
        out_shape=(jax.ShapeDtypeStruct((4, 512), f32), jax.ShapeDtypeStruct((4, 64, 1024), bf16)),
        in_specs=[hbm, vmem, vmem, vmem, vmem, hbm, vmem],
        out_specs=(vmem, vmem),
        scratch_shapes=[
            V((512, 4096), bf16), V((8, 2, 512, 256), bf16), V((2, 8, 256, 1024), bf16), V((8, 256, 1024), bf16),
            V((512, 1024), f32), V((1024, 1024), bf16), V((8, 256, 1024), f32), V((8, 256, 1024), f32),
            V((8, 256, 1024), bf16), V((2, 4, 512), jnp.int32), V((2, 8, 1024), f32),
            pltpu.SemaphoreType.DMA((2,)), pltpu.SemaphoreType.DMA((N_SEM,)), pltpu.SemaphoreType.DMA((N_SEM,)),
            *part_scratch(WIDTH[0]), *part_scratch(WIDTH[1]),
        ],
        compiler_params=pltpu.CompilerParams(
            collective_id=0, has_side_effects=True, vmem_limit_bytes=63 * 2**20
        ),
    )(
        hidden, temporal_gain[None, :], in_weight, in_scale, depth_gain[None, :],
        head_weight.reshape(256, 1024), code_ids.T,
    )
    loss, grad = pl.pallas_call(
        widen,
        out_shape=(jax.ShapeDtypeStruct((4, 512), f32), jax.ShapeDtypeStruct((4, 64, 1024), f32)),
        in_specs=[vmem, vmem],
        out_specs=(vmem, vmem),
    )(loss, grad)
    return loss.T, grad


def solution(mesh):
    in_specs = (
        P(("dp", "fsdp"), None),
        P(),
        P("fsdp", None),
        P("fsdp"),
        P(),
        P(None, "fsdp", None),
        P(("dp", "fsdp"), None),
    )
    out_specs = (P(("dp", "fsdp"), None), P(None, "fsdp", None))
    return jax.shard_map(shards, mesh=mesh, in_specs=in_specs, out_specs=out_specs, check_vma=False)
```

```python
import functools

import jax
import jax.numpy as jnp
from jax import lax
from jax.experimental import pallas as pl
from jax.experimental.pallas import tpu as pltpu
from jax.sharding import PartitionSpec as P

MESH = pl.DeviceIdType.MESH
f32, bf16 = jnp.float32, jnp.bfloat16
eps = 1e-05
cap = 30.0
loss_scale = 0.0625

Y_A, Y_B, Y_C, Y2, ZU, ZD, XQ = 0, 2, 4, 6, 8, 24, 40
GATHER = 60
SIB_W, SIB_R, SIB_S, SIB_I = 120, 128, 129, 130
RS = 131
A2, A1M, A1A, B2, B1M, B1A, S2A, S2B, S3, GZ, GX = 0, 8, 16, 24, 26, 28, 30, 33, 36, 43, 46
SUM = 58
N_SEM = RS + 2 * SUM
HOP = 4
WIDTH = (256, 256)
A_COL = (0, WIDTH[0])
B_COL = (1024 - WIDTH[0], WIDTH[0] + WIDTH[1])


def kernel(
    hidden, t_gain, weight, scale, d_gain, heads, ids,
    loss_out, grad_out,
    hid, normed, pg, ws, acc, rows, tb, eb, dl, idb, sums, lsem, ss, rs, *parts,
):
    half_parts = len(parts) // 2
    parts = (parts[:half_parts], parts[half_parts:])
    dp, fs = lax.axis_index("dp"), lax.axis_index("fsdp")
    x, y, c = dp % 4, fs // 4, fs % 2
    h, j = (fs // 2) % 2, dp // 4
    z = h * 4 + j
    par = x % 2

    def dev(px, py, pz, pc=None):
        px, py, pz = (px + 4) % 4, (py + 4) % 4, (pz + 8) % 8
        return {"dp": (pz % 4) * 4 + px, "fsdp": (py * 2 + pz // 4) * 2 + (c if pc is None else pc)}

    sib = dev(x, y, z, 1 - c)
    xd = lambda d: dev(x + d, y, z)
    yd = lambda d: dev(x, y + d, z)
    zd = lambda d: dev(x, y, z + d)

    def copy(src, dst, sem, to):
        return pltpu.make_async_remote_copy(
            src_ref=src, dst_ref=dst, send_sem=ss.at[sem], recv_sem=rs.at[sem], device_id=to, device_id_type=MESH
        )

    hid_copy = pltpu.make_async_copy(hidden, hid, lsem.at[0])
    hid_copy.start()
    own = y * 2 + h
    head_copy = pltpu.make_async_copy(heads, pg.at[1, own], lsem.at[1])
    head_copy.start()

    barrier = pltpu.get_barrier_semaphore()
    everyone = [sib] + [xd(d) for d in (1, 2, 3)] + [yd(d) for d in (1, 2, 3)] + [zd(d) for d in range(1, 8)]
    for to in everyone:
        pl.semaphore_signal(barrier, inc=1, device_id=to, device_id_type=MESH)

    on_diagonal = lax.broadcasted_iota(jnp.int32, (256, 256), 0) == lax.broadcasted_iota(jnp.int32, (256, 256), 1)
    diagonal = jnp.where(on_diagonal, scale[...].astype(f32)[None, :], 0.0).astype(bf16)
    pg[0, own] = jnp.dot(diagonal, weight[...], preferred_element_type=f32).astype(bf16)
    idb[pl.ds(c, 1)] = ids[...][None]
    pl.semaphore_wait(barrier, len(everyone))

    def slot(role):
        off = jnp.where(role % 4 == 1, 3, jnp.where(role % 4 == 2, 1, jnp.where(role % 4 == 3, 2, 0)))
        return ((y + off) % 4) * 2 + jnp.where(role < 4, h, 1 - h)

    def piece(m, role, start, count):
        return pg.at[m, slot(role), pl.ds(pl.multiple_of(start, 16), count)]

    q0, q1, rest = par * 128, par * 128 + 64, (1 - par) * 128
    o0, o1 = (1 - par) * 128, (1 - par) * 128 + 64

    def move(m, role, start, count, sem, to):
        ref = piece(m, role, start, count)
        return copy(ref, ref, m * GATHER + sem, to)

    def y_send(m, sem):
        plus, minus, count = {Y_A: (q0, q1, 64), Y_B: (q1, q0, 64), Y_C: (rest, rest, 128)}[sem]
        move(m, 0, plus, count, sem, yd(1)).start()
        move(m, 0, minus, count, sem + 1, yd(-1)).start()

    def z_up(m, k, sub):
        return move(m, k, q0 + 16 * sub, 16, ZU + 4 * (k % 4) + sub, zd(1))

    def z_down(m, k, sub):
        return move(m, k, q1 + 16 * sub, 16, ZD + 4 * (k % 4) + sub, zd(-1))

    def y_sent(m, sem):
        move(m, 0, 0, 64, sem, yd(1)).wait_send()
        move(m, 0, 0, 64, sem + 1, yd(-1)).wait_send()

    def up_source(m, k):
        @pl.when(j == 3)
        def _():
            for sub in range(4):
                z_up(m, k, sub).start()

    def down_source(m, k):
        @pl.when(j == 0)
        def _():
            for sub in range(4):
                z_down(m, k, sub).start()

    def x_up(m, role, half):
        return move(m, role, q0 + 32 * half, 32, XQ + 4 * (role - 3) + 2 * half, xd(1))

    def x_down(m, role, half):
        return move(m, role, q1 + 32 * half, 32, XQ + 4 * (role - 3) + 2 * half + 1, xd(-1))

    def y_first(m):
        move(m, 1, q0, 64, Y_A, yd(1)).wait_recv()
        move(m, 1, q0, 64, Y2, yd(1)).start()
        up_source(m, 1)
        move(m, 2, q1, 64, Y_A + 1, yd(-1)).wait_recv()
        move(m, 2, q1, 64, Y2 + 1, yd(-1)).start()
        down_source(m, 2)

    def y_second(m):
        move(m, 1, q1, 64, Y_B, yd(1)).wait_recv()
        down_source(m, 1)
        move(m, 2, q0, 64, Y_B + 1, yd(-1)).wait_recv()
        up_source(m, 2)

    def y_rest(m):
        move(m, 1, rest, 128, Y_C, yd(1)).wait_recv()
        move(m, 2, rest, 128, Y_C + 1, yd(-1)).wait_recv()

    def y_far(m):
        move(m, 3, q0, 64, Y2, yd(1)).wait_recv()
        up_source(m, 3)
        x_up(m, 3, 0).start()
        x_up(m, 3, 1).start()
        move(m, 3, q1, 64, Y2 + 1, yd(-1)).wait_recv()
        down_source(m, 3)
        x_down(m, 3, 0).start()
        x_down(m, 3, 1).start()

    def z_piece(i, first):
        q = i // 4
        k = jnp.where(q < 2, 0, jnp.where(q < 5, q - 1, q - 4))
        k = jnp.where(k == 1, first, jnp.where(k == 2, 3 - first, k))
        return jnp.where(jnp.logical_or(q == 1, q >= 5), 1, 0), 4 + k, i % 4

    def z_one(n):
        up, down = n - HOP * j, n - HOP * (3 - j)

        @pl.when(jnp.logical_and(up >= 0, up < 32))
        def _():
            m, role, sub = z_piece(up, 1)
            z_up(m, role, sub).wait_recv()

            @pl.when(j < 3)
            def _():
                z_up(m, role, sub).start()

            @pl.when(sub % 2 == 1)
            def _():
                x_up(m, role, sub // 2).start()

        @pl.when(jnp.logical_and(down >= 0, down < 32))
        def _():
            m, role, sub = z_piece(down, 2)
            z_down(m, role, sub).wait_recv()

            @pl.when(j > 0)
            def _():
                z_down(m, role, sub).start()

            @pl.when(sub % 2 == 1)
            def _():
                x_down(m, role, sub // 2).start()

    def z_step(n):
        @pl.loop(2 * n, 2 * n + 2)
        def _(i):
            z_one(i)

    def x_wait(m, role):
        for half in range(2):
            sem = XQ + 4 * (role - 3) + 2 * half
            move(m, role, o0 + 32 * half, 32, sem, xd(1)).wait_recv()
            move(m, role, o1 + 32 * half, 32, sem + 1, xd(-1)).wait_recv()

    def to_sibling(role):
        s = slot(role)
        return copy(pg.at[0, s], ws.at[s], SIB_W + role, sib)

    def project(role):
        to_sibling(role).wait_recv()
        s = slot(role)

        acc[...] += jnp.dot(normed[s, c], pg[0, s], preferred_element_type=f32) + jnp.dot(
            normed[s, 1 - c], ws[s], preferred_element_type=f32
        )

    y_send(0, Y_A)
    up_source(0, 0)
    down_source(0, 0)
    to_sibling(0).start()
    id_copy = copy(idb.at[c], idb.at[c], SIB_I, sib)
    id_copy.start()
    head_copy.wait()
    up_source(1, 0)
    down_source(1, 0)
    acc[...] = jnp.zeros_like(acc)
    sums[...] = jnp.zeros_like(sums)
    hid_copy.wait()

    def norm(part):
        at = pl.ds(part * 64, 64)
        block = hid[at, :].astype(f32)
        inv = lax.rsqrt(jnp.mean(block * block, axis=-1, keepdims=True) + eps)
        out = (block * inv * t_gain[...]).astype(bf16)
        for s in range(16):
            normed[s // 2, s % 2, at, :] = out[:, s * 256 : (s + 1) * 256]

    norm(0)
    norm(1)
    y_sent(0, Y_A)
    y_send(0, Y_B)
    z_step(0)
    y_first(0)
    z_step(1)
    norm(2)
    z_step(2)
    y_sent(0, Y_B)
    y_send(1, Y_A)
    z_step(3)
    y_second(0)
    z_step(4)
    norm(3)
    z_step(5)
    y_far(0)
    y_sent(1, Y_A)
    y_send(1, Y_B)
    z_step(6)
    y_first(1)
    norm(4)
    z_step(7)
    z_step(8)
    y_sent(1, Y_B)
    y_second(1)
    norm(5)
    z_step(9)
    z_step(10)
    y_far(1)
    y_send(0, Y_C)
    norm(6)
    z_step(11)
    norm(7)
    z_step(12)
    z_step(13)
    x_wait(0, 3)
    to_sibling(3).start()
    project(0)
    z_step(14)
    x_wait(0, 4)
    to_sibling(4).start()
    z_step(15)
    project(3)
    y_send(1, Y_C)
    z_step(16)
    project(4)
    z_step(17)
    z_step(18)
    y_rest(0)
    to_sibling(1).start()
    to_sibling(2).start()
    z_step(19)
    x_wait(0, 5)
    to_sibling(5).start()
    project(1)
    x_wait(0, 6)
    to_sibling(6).start()
    z_step(20)
    project(2)
    project(5)
    z_step(21)
    project(6)
    x_wait(0, 7)
    to_sibling(7).start()
    project(7)

    @pl.loop(0, 2)
    def _(r):
        block = acc[pl.ds(pl.multiple_of(r * 256, 256), 256), :]
        inv = lax.rsqrt(jnp.mean(block * block, axis=-1, keepdims=True) + eps)
        rows[pl.ds(pl.multiple_of(c * 512 + r * 256, 256), 256), :] = (block * inv * d_gain[...]).astype(bf16)

    my_rows = rows.at[pl.ds(pl.multiple_of(c * 512, 512), 512)]
    row_copy = copy(my_rows, my_rows, SIB_R, sib)
    row_copy.start()
    id_copy.wait_recv()
    y_rest(1)
    for role in range(3, 8):
        x_wait(1, role)

    def score(n):
        cols = pl.ds(pl.multiple_of(n * 256, 256), 256)
        ids_at = idb[n // 2, :, pl.ds(pl.multiple_of((n % 2) * 256, 256), 256)]
        for b in range(8):
            got = lax.dot_general(
                pg[1, b], rows[cols, :], (((1,), (1,)), ((), ())), preferred_element_type=f32
            )
            card = lax.broadcasted_iota(jnp.int32, (64, 256), 0) + (b * 2 + c) * 64
            for k in range(4):
                part = slice(k * 64, (k + 1) * 64)
                t = jnp.tanh(got[part] * (1.0 / cap))
                e = jnp.exp(t * cap)
                tb[b, part, cols] = t
                eb[b, part, cols] = e
                hit = card == ids_at[k : k + 1, :]
                sums[c, k : k + 1, cols] += jnp.sum(e, axis=0, keepdims=True)
                sums[c, k + 4 : k + 5, cols] += jnp.sum(jnp.where(hit, t, 0.0), axis=0, keepdims=True)

    @pl.loop(0, 2)
    def _(n):
        score(c * 2 + n)

    row_copy.wait_recv()

    @pl.loop(0, 2)
    def _(n):
        score((1 - c) * 2 + n)

    my_sums = sums.at[c]
    sum_copy = copy(my_sums, my_sums, SIB_S, sib)
    sum_copy.start()
    sum_copy.wait_recv()
    totals = sums[0, 0:4, :] + sums[1, 0:4, :]
    mine_f = pl.ds(pl.multiple_of(c * 512, 512), 512)
    loss_out[...] = jnp.log(sums[0, 0:4, mine_f] + sums[1, 0:4, mine_f]) - cap * (
        sums[0, 4:8, mine_f] + sums[1, 4:8, mine_f]
    )
    sum_copy.wait_send()
    sums[c, 0:4, :] = 1.0 / totals

    def logits(b):
        @pl.loop(0, 4)
        def _(n):
            cols = pl.ds(pl.multiple_of(n * 256, 256), 256)
            ids_at = idb[n // 2, :, pl.ds(pl.multiple_of((n % 2) * 256, 256), 256)]
            card = lax.broadcasted_iota(jnp.int32, (64, 256), 0) + (b * 2 + c) * 64
            for k in range(4):
                part = slice(k * 64, (k + 1) * 64)
                t = tb[b, part, cols]
                p = eb[b, part, cols] * sums[c, k : k + 1, cols]
                hit = card == ids_at[k : k + 1, :]
                p = jnp.where(hit, p - 1.0, p)
                dl[b, part, cols] = (p * ((1.0 - t * t) * loss_scale)).astype(bf16)

    head = lambda d: pl.ds(pl.multiple_of(((x + d + 4) % 4) * 64, 64), 64)
    my_head = head(0)
    strip = pl.ds(pl.multiple_of(j * 16, 16), 16)

    class Part:
        def __init__(self, q):
            self.w, self.a, self.b, self.base = WIDTH[q], A_COL[q], B_COL[q], RS + q * SUM
            (self.ga, self.gb, self.ra2, self.ra1m, self.ra1a, self.saa, self.rb2, self.rb1m, self.rb1a, self.sab,
             self.sa, self.sb, self.s2a, self.r2a, self.s2b, self.r2b, self.tt, self.s3, self.r3, self.fin) = parts[q]

        def send(self, src, dst, sem, to):
            return copy(src, dst, self.base + sem, to)

        def gradient(self, i):
            b0 = ((y + jnp.where(i == 0, 2, jnp.where(i == 1, 1, jnp.where(i == 2, 3, 0)))) % 4) * 2
            logits(b0)
            logits(b0 + 1)
            both = pl.ds(b0, 2)
            for col, out in ((self.a, self.ga), (self.b, self.gb)):
                g = jnp.dot(
                    dl[both].reshape(512, 1024), rows[:, col : col + self.w], preferred_element_type=f32
                ).reshape(2, 256, self.w)
                eb[both, :, col : col + self.w] = g
                out[both] = g.astype(bf16)
            for hp in range(2):
                b = b0 + hp
                self.leave(b, hp)

                @pl.when(i == 0)
                def _():
                    self.far_b(b, hp)

                @pl.when(i == 2 - hp)
                def _():
                    self.near_b(b, hp)

        def gradient_rest(self):
            g = jnp.dot(
                dl[...].reshape(2048, 1024), rows[:, self.a : self.a + 2 * self.w], preferred_element_type=f32
            ).reshape(8, 256, 2 * self.w)
            eb[:, :, self.a : self.a + 2 * self.w] = g
            self.ga[...] = g[:, :, : self.w].astype(bf16)
            self.gb[...] = g[:, :, self.w :].astype(bf16)
            for hp in range(2):
                s = 1 - 2 * hp
                self.far_b(((y + 2) % 4) * 2 + hp, hp)
                self.near_b(((y - s + 4) % 4) * 2 + hp, hp)
            for b in range(8):
                self.leave(b, b % 2)

        def leave(self, b, hp):
            s = 1 - 2 * hp
            self.send(self.ga.at[b, head(2)], self.ra2.at[b], A2 + b, xd(s)).start()
            self.send(self.ga.at[b, head(-s)], self.ra1m.at[b], A1M + b, xd(-s)).start()

        def far_b(self, b, hp):
            self.send(self.gb.at[b], self.rb2.at[hp], B2 + hp, yd(1 - 2 * hp)).start()

        def near_b(self, b, hp):
            self.send(self.gb.at[b], self.rb1m.at[hp], B1M + hp, yd(2 * hp - 1)).start()

        def ride(self):
            for hp in range(2):
                s = 1 - 2 * hp
                b = ((y + s + 4) % 4) * 2 + hp
                self.send(self.sab.at[hp], self.rb2.at[hp], B2 + hp, yd(s)).wait_recv()
                for r in range(4):
                    at = slice(r * 64, (r + 1) * 64)
                    self.sab[hp, at, :] = (
                        eb[b, at, self.b : self.b + self.w] + self.rb2[hp, at, :].astype(f32)
                    ).astype(bf16)
                self.send(self.sab.at[hp], self.rb1a.at[hp], B1A + hp, yd(s)).start()

            @pl.loop(0, 8)
            def _(b):
                s = 1 - 2 * (b % 2)
                self.send(self.saa.at[b], self.ra2.at[b], A2 + b, xd(s)).wait_recv()
                self.saa[b] = (eb[b, head(s), self.a : self.a + self.w] + self.ra2[b].astype(f32)).astype(bf16)
                self.send(self.saa.at[b], self.ra1a.at[b], A1A + b, xd(s)).start()

        def first(self):
            for hp in range(2):
                s = 1 - 2 * hp
                self.send(self.sab.at[hp], self.rb1m.at[hp], B1M + hp, yd(-s)).wait_recv()
                self.send(self.sab.at[hp], self.rb1a.at[hp], B1A + hp, yd(s)).wait_recv()
                for r in range(4):
                    at = slice(r * 64, (r + 1) * 64)
                    self.sb[hp, at, :] = (
                        eb[y * 2 + hp, at, self.b : self.b + self.w]
                        + self.rb1m[hp, at, :].astype(f32)
                        + self.rb1a[hp, at, :].astype(f32)
                    )
            for d in (2, 1, 3):
                self.s2b[d - 1] = self.sb[:, head(d), :].astype(bf16)
                self.send(self.s2b.at[d - 1], self.r2b.at[d - 1], S2B + d - 1, xd(d)).start()

            @pl.loop(0, 8)
            def _(b):
                s = 1 - 2 * (b % 2)
                self.send(self.saa.at[b], self.ra1m.at[b], A1M + b, xd(-s)).wait_recv()
                self.send(self.saa.at[b], self.ra1a.at[b], A1A + b, xd(s)).wait_recv()
                self.sa[b] = (
                    eb[b, my_head, self.a : self.a + self.w] + self.ra1m[b].astype(f32) + self.ra1a[b].astype(f32)
                )

            for d in (2, 1, 3):
                self.s2a[d - 1] = self.sa[pl.ds(((y + d) % 4) * 2, 2)].astype(bf16)
                self.send(self.s2a.at[d - 1], self.r2a.at[d - 1], S2A + d - 1, yd(d)).start()

        def second(self):
            w = self.w
            for d in range(3):
                self.send(self.s2b.at[d], self.r2b.at[d], S2B + d, xd(d + 1)).wait_recv()
            self.tt[:, :, w:] = (
                self.sb[:, my_head, :]
                + self.r2b[0].astype(f32) + self.r2b[1].astype(f32) + self.r2b[2].astype(f32)
            )
            for d in range(3):
                self.send(self.s2a.at[d], self.r2a.at[d], S2A + d, yd(d + 1)).wait_recv()
            self.tt[:, :, :w] = (
                self.sa[pl.ds(y * 2, 2)]
                + self.r2a[0].astype(f32) + self.r2a[1].astype(f32) + self.r2a[2].astype(f32)
            )
            self.s3[...] = self.tt[...].astype(bf16)
            for d in (4, 3, 5, 2, 6, 1, 7):
                to = (z + d) % 8
                at = pl.ds(pl.multiple_of((to % 4) * 16, 16), 16)
                self.send(self.s3.at[to // 4, at], self.r3.at[d - 1], S3 + d - 1, zd(d)).start()

        def z_share(self, d):
            here = self.fin.at[x, strip]
            return self.send(here, here, GZ + d - 1, dev(x, y, h * 4 + (j + d) % 4))

        def x_share(self, e, d):
            here = self.fin.at[x, pl.ds(pl.multiple_of(((j + 4 - e) % 4) * 16, 16), 16)]
            return self.send(here, here, GX + 3 * e + d - 1, xd(d))

        def third(self):
            total = self.tt[h, strip, :]
            for d in (1, 7, 2, 6, 3, 5, 4):
                self.send(self.r3.at[d - 1], self.r3.at[d - 1], S3 + d - 1, zd(d)).wait_recv()
                total = total + self.r3[d - 1].astype(f32)
            self.fin[x, strip, :] = total.astype(bf16)
            for d in (2, 1, 3):
                self.z_share(d).start()
            for d in (2, 1, 3):
                self.x_share(0, d).start()

        def share(self):
            for e in (1, 3, 2):
                self.z_share(e).wait_recv()
                for d in (2, 1, 3):
                    self.x_share(e, d).start()
            self.store(x)

        def store(self, k):
            grad_out[k, :, self.a : self.a + self.w] = self.fin[k, :, : self.w]
            grad_out[k, :, self.b : self.b + self.w] = self.fin[k, :, self.w :]

        def finish(self):
            for d in (1, 3, 2):
                for e in (0, 1, 3, 2):
                    self.x_share(e, d).wait_recv()
                self.store((x + 4 - d) % 4)

        def sent(self):
            for b in range(8):
                for sem in (A2, A1M, A1A):
                    self.send(self.saa.at[b], self.ra2.at[b], sem + b, sib).wait_send()
            for hp in range(2):
                for sem in (B2, B1M, B1A):
                    self.send(self.sab.at[hp], self.rb2.at[hp], sem + hp, sib).wait_send()
            for d in range(3):
                self.send(self.s2a.at[d], self.r2a.at[d], S2A + d, sib).wait_send()
                self.send(self.s2b.at[d], self.r2b.at[d], S2B + d, sib).wait_send()
                self.z_share(d + 1).wait_send()
                for e in range(4):
                    self.x_share(e, d + 1).wait_send()
            for d in range(7):
                self.send(self.r3.at[d], self.r3.at[d], S3 + d, sib).wait_send()

    one, two = Part(0), Part(1)

    @pl.loop(0, 4)
    def _(i):
        one.gradient(i)

    two.gradient_rest()

    one.ride()
    two.ride()
    one.first()
    two.first()
    one.second()
    two.second()
    one.third()
    two.third()
    one.share()
    two.share()
    one.finish()
    two.finish()

    for m in range(2):
        for sem, count in ((Y_C, 128), (Y_C + 1, 128)):
            move(m, 0, 0, count, sem, yd(1)).wait_send()
        for sem in (Y2, Y2 + 1):
            move(m, 0, 0, 64, sem, yd(1)).wait_send()
        for sem in range(ZU, XQ):
            move(m, 0, 0, 16, sem, yd(1)).wait_send()
        for sem in range(XQ, GATHER):
            move(m, 0, 0, 32, sem, yd(1)).wait_send()
    for role in range(8):
        to_sibling(role).wait_send()
    row_copy.wait_send()
    id_copy.wait_send()
    one.sent()
    two.sent()


def widen(loss, grad, loss_out, grad_out):
    loss_out[...] = loss[...]
    grad_out[...] = grad[...].astype(f32)


def part_scratch(w):
    shapes = (
        [((8, 256, w), bf16)] * 2 + [((8, 64, w), bf16)] * 4 + [((2, 256, w), bf16)] * 4
        + [((8, 64, w), f32), ((2, 256, w), f32)] + [((3, 2, 64, w), bf16)] * 4
        + [((2, 64, 2 * w), f32), ((2, 64, 2 * w), bf16), ((7, 16, 2 * w), bf16), ((4, 64, 2 * w), bf16)]
    )
    return [pltpu.VMEM(shape, kind) for shape, kind in shapes]


def shards(hidden, temporal_gain, in_weight, in_scale, depth_gain, head_weight, code_ids):
    vmem = pl.BlockSpec(memory_space=pltpu.VMEM)
    hbm = pl.BlockSpec(memory_space=pl.ANY)
    V = pltpu.VMEM
    loss, grad = pl.pallas_call(
        kernel,
        out_shape=(jax.ShapeDtypeStruct((4, 512), f32), jax.ShapeDtypeStruct((4, 64, 1024), bf16)),
        in_specs=[hbm, vmem, vmem, vmem, vmem, hbm, vmem],
        out_specs=(vmem, vmem),
        scratch_shapes=[
            V((512, 4096), bf16), V((8, 2, 512, 256), bf16), V((2, 8, 256, 1024), bf16), V((8, 256, 1024), bf16),
            V((512, 1024), f32), V((1024, 1024), bf16), V((8, 256, 1024), f32), V((8, 256, 1024), f32),
            V((8, 256, 1024), bf16), V((2, 4, 512), jnp.int32), V((2, 8, 1024), f32),
            pltpu.SemaphoreType.DMA((2,)), pltpu.SemaphoreType.DMA((N_SEM,)), pltpu.SemaphoreType.DMA((N_SEM,)),
            *part_scratch(WIDTH[0]), *part_scratch(WIDTH[1]),
        ],
        compiler_params=pltpu.CompilerParams(
            collective_id=0, has_side_effects=True, vmem_limit_bytes=63 * 2**20
        ),
    )(
        hidden, temporal_gain[None, :], in_weight, in_scale, depth_gain[None, :],
        head_weight.reshape(256, 1024), code_ids.T,
    )
    loss, grad = pl.pallas_call(
        widen,
        out_shape=(jax.ShapeDtypeStruct((4, 512), f32), jax.ShapeDtypeStruct((4, 64, 1024), f32)),
        in_specs=[vmem, vmem],
        out_specs=(vmem, vmem),
    )(loss, grad)
    return loss.T, grad


def solution(mesh):
    in_specs = (
        P(("dp", "fsdp"), None),
        P(),
        P("fsdp", None),
        P("fsdp"),
        P(),
        P(None, "fsdp", None),
        P(("dp", "fsdp"), None),
    )
    out_specs = (P(("dp", "fsdp"), None), P(None, "fsdp", None))
    return jax.shard_map(shards, mesh=mesh, in_specs=in_specs, out_specs=out_specs, check_vma=False)
```

```python
import functools

import jax
import jax.numpy as jnp
from jax import lax
from jax.experimental import pallas as pl
from jax.experimental.pallas import tpu as pltpu
from jax.sharding import PartitionSpec as P

MESH = pl.DeviceIdType.MESH
f32, bf16 = jnp.float32, jnp.bfloat16
eps = 1e-05
cap = 30.0
loss_scale = 0.0625

Y_A, Y_B, Y_C, Y2, ZU, ZD, XQ = 0, 2, 4, 6, 8, 24, 40
GATHER = 60
SIB_W, SIB_R, SIB_S, SIB_I = 120, 128, 129, 130
RS = 131
A2, A1M, A1A, B2, B1M, B1A, S2A, S2B, S3, GZ, GX = 0, 8, 16, 24, 26, 28, 30, 33, 36, 43, 46
SUM = 58
N_SEM = RS + 2 * SUM
HOP = 4
WIDTH = (256, 256)
A_COL = (0, WIDTH[0])
B_COL = (1024 - WIDTH[0], WIDTH[0] + WIDTH[1])


def kernel(
    hidden, t_gain, weight, scale, d_gain, heads, ids,
    loss_out, grad_out,
    wbuf, hid, normed, pg, ws, acc, rows, tb, eb, dl, idb, sums, lsem, ss, rs, *parts,
):
    half_parts = len(parts) // 2
    parts = (parts[:half_parts], parts[half_parts:])
    dp, fs = lax.axis_index("dp"), lax.axis_index("fsdp")
    x, y, c = dp % 4, fs // 4, fs % 2
    h, j = (fs // 2) % 2, dp // 4
    z = h * 4 + j
    par = x % 2

    def dev(px, py, pz, pc=None):
        px, py, pz = (px + 4) % 4, (py + 4) % 4, (pz + 8) % 8
        return {"dp": (pz % 4) * 4 + px, "fsdp": (py * 2 + pz // 4) * 2 + (c if pc is None else pc)}

    sib = dev(x, y, z, 1 - c)
    xd = lambda d: dev(x + d, y, z)
    yd = lambda d: dev(x, y + d, z)
    zd = lambda d: dev(x, y, z + d)

    def copy(src, dst, sem, to):
        return pltpu.make_async_remote_copy(
            src_ref=src, dst_ref=dst, send_sem=ss.at[sem], recv_sem=rs.at[sem], device_id=to, device_id_type=MESH
        )

    barrier = pltpu.get_barrier_semaphore()
    everyone = [sib] + [xd(d) for d in (1, 2, 3)] + [yd(d) for d in (1, 2, 3)] + [zd(d) for d in range(1, 8)]
    for to in everyone:
        pl.semaphore_signal(barrier, inc=1, device_id=to, device_id_type=MESH)

    weight_copy = pltpu.make_async_copy(weight, wbuf, lsem.at[2])
    weight_copy.start()
    hid_copy = pltpu.make_async_copy(hidden, hid, lsem.at[0])
    hid_copy.start()
    own = y * 2 + h
    head_copy = pltpu.make_async_copy(heads, pg.at[1, own], lsem.at[1])
    head_copy.start()

    on_diagonal = lax.broadcasted_iota(jnp.int32, (256, 256), 0) == lax.broadcasted_iota(jnp.int32, (256, 256), 1)
    diagonal = jnp.where(on_diagonal, scale[...].astype(f32)[None, :], 0.0).astype(bf16)
    weight_copy.wait()
    pg[0, own] = jnp.dot(diagonal, wbuf[...], preferred_element_type=f32).astype(bf16)
    idb[pl.ds(c, 1)] = ids[...][None]
    pl.semaphore_wait(barrier, len(everyone))

    def slot(role):
        off = jnp.where(role % 4 == 1, 3, jnp.where(role % 4 == 2, 1, jnp.where(role % 4 == 3, 2, 0)))
        return ((y + off) % 4) * 2 + jnp.where(role < 4, h, 1 - h)

    def piece(m, role, start, count):
        return pg.at[m, slot(role), pl.ds(pl.multiple_of(start, 16), count)]

    q0, q1, rest = par * 128, par * 128 + 64, (1 - par) * 128
    o0, o1 = (1 - par) * 128, (1 - par) * 128 + 64

    def move(m, role, start, count, sem, to):
        ref = piece(m, role, start, count)
        return copy(ref, ref, m * GATHER + sem, to)

    def y_send(m, sem):
        plus, minus, count = {Y_A: (q0, q1, 64), Y_B: (q1, q0, 64), Y_C: (rest, rest, 128)}[sem]
        move(m, 0, plus, count, sem, yd(1)).start()
        move(m, 0, minus, count, sem + 1, yd(-1)).start()

    def z_up(m, k, sub):
        return move(m, k, q0 + 16 * sub, 16, ZU + 4 * (k % 4) + sub, zd(1))

    def z_down(m, k, sub):
        return move(m, k, q1 + 16 * sub, 16, ZD + 4 * (k % 4) + sub, zd(-1))

    def y_sent(m, sem):
        move(m, 0, 0, 64, sem, yd(1)).wait_send()
        move(m, 0, 0, 64, sem + 1, yd(-1)).wait_send()

    def up_source(m, k):
        @pl.when(j == 3)
        def _():
            for sub in range(4):
                z_up(m, k, sub).start()

    def down_source(m, k):
        @pl.when(j == 0)
        def _():
            for sub in range(4):
                z_down(m, k, sub).start()

    def x_up(m, role, half):
        return move(m, role, q0 + 32 * half, 32, XQ + 4 * (role - 3) + 2 * half, xd(1))

    def x_down(m, role, half):
        return move(m, role, q1 + 32 * half, 32, XQ + 4 * (role - 3) + 2 * half + 1, xd(-1))

    def y_first(m):
        move(m, 1, q0, 64, Y_A, yd(1)).wait_recv()
        move(m, 1, q0, 64, Y2, yd(1)).start()
        up_source(m, 1)
        move(m, 2, q1, 64, Y_A + 1, yd(-1)).wait_recv()
        move(m, 2, q1, 64, Y2 + 1, yd(-1)).start()
        down_source(m, 2)

    def y_second(m):
        move(m, 1, q1, 64, Y_B, yd(1)).wait_recv()
        down_source(m, 1)
        move(m, 2, q0, 64, Y_B + 1, yd(-1)).wait_recv()
        up_source(m, 2)

    def y_rest(m):
        move(m, 1, rest, 128, Y_C, yd(1)).wait_recv()
        move(m, 2, rest, 128, Y_C + 1, yd(-1)).wait_recv()

    def y_far(m):
        move(m, 3, q0, 64, Y2, yd(1)).wait_recv()
        up_source(m, 3)
        x_up(m, 3, 0).start()
        x_up(m, 3, 1).start()
        move(m, 3, q1, 64, Y2 + 1, yd(-1)).wait_recv()
        down_source(m, 3)
        x_down(m, 3, 0).start()
        x_down(m, 3, 1).start()

    def z_piece(i, first):
        q = i // 4
        k = jnp.where(q < 2, 0, jnp.where(q < 5, q - 1, q - 4))
        k = jnp.where(k == 1, first, jnp.where(k == 2, 3 - first, k))
        return jnp.where(jnp.logical_or(q == 1, q >= 5), 1, 0), 4 + k, i % 4

    def z_one(n):
        up, down = n - HOP * j, n - HOP * (3 - j)

        @pl.when(jnp.logical_and(up >= 0, up < 32))
        def _():
            m, role, sub = z_piece(up, 1)
            z_up(m, role, sub).wait_recv()

            @pl.when(j < 3)
            def _():
                z_up(m, role, sub).start()

            @pl.when(sub % 2 == 1)
            def _():
                x_up(m, role, sub // 2).start()

        @pl.when(jnp.logical_and(down >= 0, down < 32))
        def _():
            m, role, sub = z_piece(down, 2)
            z_down(m, role, sub).wait_recv()

            @pl.when(j > 0)
            def _():
                z_down(m, role, sub).start()

            @pl.when(sub % 2 == 1)
            def _():
                x_down(m, role, sub // 2).start()

    def z_step(n):
        @pl.loop(2 * n, 2 * n + 2)
        def _(i):
            z_one(i)

    def x_wait(m, role):
        for half in range(2):
            sem = XQ + 4 * (role - 3) + 2 * half
            move(m, role, o0 + 32 * half, 32, sem, xd(1)).wait_recv()
            move(m, role, o1 + 32 * half, 32, sem + 1, xd(-1)).wait_recv()

    def to_sibling(role):
        s = slot(role)
        return copy(pg.at[0, s], ws.at[s], SIB_W + role, sib)

    def project(role):
        to_sibling(role).wait_recv()
        s = slot(role)

        acc[...] += jnp.dot(normed[s, c], pg[0, s], preferred_element_type=f32) + jnp.dot(
            normed[s, 1 - c], ws[s], preferred_element_type=f32
        )

    y_send(0, Y_A)
    up_source(0, 0)
    down_source(0, 0)
    to_sibling(0).start()
    id_copy = copy(idb.at[c], idb.at[c], SIB_I, sib)
    id_copy.start()
    head_copy.wait()
    up_source(1, 0)
    down_source(1, 0)
    acc[...] = jnp.zeros_like(acc)
    sums[...] = jnp.zeros_like(sums)
    hid_copy.wait()

    def norm(part):
        at = pl.ds(part * 64, 64)
        block = hid[at, :].astype(f32)
        inv = lax.rsqrt(jnp.mean(block * block, axis=-1, keepdims=True) + eps)
        out = (block * inv * t_gain[...]).astype(bf16)
        for s in range(16):
            normed[s // 2, s % 2, at, :] = out[:, s * 256 : (s + 1) * 256]

    norm(0)
    norm(1)
    y_sent(0, Y_A)
    y_send(0, Y_B)
    z_step(0)
    y_first(0)
    z_step(1)
    norm(2)
    z_step(2)
    y_sent(0, Y_B)
    y_send(1, Y_A)
    z_step(3)
    y_second(0)
    z_step(4)
    norm(3)
    z_step(5)
    y_far(0)
    y_sent(1, Y_A)
    y_send(1, Y_B)
    z_step(6)
    y_first(1)
    norm(4)
    z_step(7)
    z_step(8)
    y_sent(1, Y_B)
    y_second(1)
    norm(5)
    z_step(9)
    z_step(10)
    y_far(1)
    y_send(0, Y_C)
    norm(6)
    z_step(11)
    norm(7)
    z_step(12)
    z_step(13)
    x_wait(0, 3)
    to_sibling(3).start()
    project(0)
    z_step(14)
    x_wait(0, 4)
    to_sibling(4).start()
    z_step(15)
    project(3)
    y_send(1, Y_C)
    z_step(16)
    project(4)
    z_step(17)
    z_step(18)
    y_rest(0)
    to_sibling(1).start()
    to_sibling(2).start()
    z_step(19)
    x_wait(0, 5)
    to_sibling(5).start()
    project(1)
    x_wait(0, 6)
    to_sibling(6).start()
    z_step(20)
    project(2)
    project(5)
    z_step(21)
    project(6)
    x_wait(0, 7)
    to_sibling(7).start()
    project(7)

    @pl.loop(0, 2)
    def _(r):
        block = acc[pl.ds(pl.multiple_of(r * 256, 256), 256), :]
        inv = lax.rsqrt(jnp.mean(block * block, axis=-1, keepdims=True) + eps)
        rows[pl.ds(pl.multiple_of(c * 512 + r * 256, 256), 256), :] = (block * inv * d_gain[...]).astype(bf16)

    my_rows = rows.at[pl.ds(pl.multiple_of(c * 512, 512), 512)]
    row_copy = copy(my_rows, my_rows, SIB_R, sib)
    row_copy.start()
    id_copy.wait_recv()
    y_rest(1)
    for role in range(3, 8):
        x_wait(1, role)

    def score(n):
        cols = pl.ds(pl.multiple_of(n * 256, 256), 256)
        ids_at = idb[n // 2, :, pl.ds(pl.multiple_of((n % 2) * 256, 256), 256)]
        for b in range(8):
            got = lax.dot_general(
                pg[1, b], rows[cols, :], (((1,), (1,)), ((), ())), preferred_element_type=f32
            )
            card = lax.broadcasted_iota(jnp.int32, (64, 256), 0) + (b * 2 + c) * 64
            for k in range(4):
                part = slice(k * 64, (k + 1) * 64)
                t = jnp.tanh(got[part] * (1.0 / cap))
                e = jnp.exp(t * cap)
                tb[b, part, cols] = t
                eb[b, part, cols] = e
                hit = card == ids_at[k : k + 1, :]
                sums[c, k : k + 1, cols] += jnp.sum(e, axis=0, keepdims=True)
                sums[c, k + 4 : k + 5, cols] += jnp.sum(jnp.where(hit, t, 0.0), axis=0, keepdims=True)

    @pl.loop(0, 2)
    def _(n):
        score(c * 2 + n)

    row_copy.wait_recv()

    @pl.loop(0, 2)
    def _(n):
        score((1 - c) * 2 + n)

    my_sums = sums.at[c]
    sum_copy = copy(my_sums, my_sums, SIB_S, sib)
    sum_copy.start()
    sum_copy.wait_recv()
    totals = sums[0, 0:4, :] + sums[1, 0:4, :]
    mine_f = pl.ds(pl.multiple_of(c * 512, 512), 512)
    loss_out[...] = jnp.log(sums[0, 0:4, mine_f] + sums[1, 0:4, mine_f]) - cap * (
        sums[0, 4:8, mine_f] + sums[1, 4:8, mine_f]
    )
    sum_copy.wait_send()
    sums[c, 0:4, :] = 1.0 / totals

    def logits(b):
        @pl.loop(0, 4)
        def _(n):
            cols = pl.ds(pl.multiple_of(n * 256, 256), 256)
            ids_at = idb[n // 2, :, pl.ds(pl.multiple_of((n % 2) * 256, 256), 256)]
            card = lax.broadcasted_iota(jnp.int32, (64, 256), 0) + (b * 2 + c) * 64
            for k in range(4):
                part = slice(k * 64, (k + 1) * 64)
                t = tb[b, part, cols]
                p = eb[b, part, cols] * sums[c, k : k + 1, cols]
                hit = card == ids_at[k : k + 1, :]
                p = jnp.where(hit, p - 1.0, p)
                dl[b, part, cols] = (p * ((1.0 - t * t) * loss_scale)).astype(bf16)

    head = lambda d: pl.ds(pl.multiple_of(((x + d + 4) % 4) * 64, 64), 64)
    my_head = head(0)
    strip = pl.ds(pl.multiple_of(j * 16, 16), 16)

    class Part:
        def __init__(self, q):
            self.w, self.a, self.b, self.base = WIDTH[q], A_COL[q], B_COL[q], RS + q * SUM
            (self.ga, self.gb, self.ra2, self.ra1m, self.ra1a, self.saa, self.rb2, self.rb1m, self.rb1a, self.sab,
             self.sa, self.sb, self.s2a, self.r2a, self.s2b, self.r2b, self.tt, self.s3, self.r3, self.fin) = parts[q]

        def send(self, src, dst, sem, to):
            return copy(src, dst, self.base + sem, to)

        def gradient(self, i):
            b0 = ((y + jnp.where(i == 0, 2, jnp.where(i == 1, 1, jnp.where(i == 2, 3, 0)))) % 4) * 2
            logits(b0)
            logits(b0 + 1)
            both = pl.ds(b0, 2)
            for col, out in ((self.a, self.ga), (self.b, self.gb)):
                g = jnp.dot(
                    dl[both].reshape(512, 1024), rows[:, col : col + self.w], preferred_element_type=f32
                ).reshape(2, 256, self.w)
                eb[both, :, col : col + self.w] = g
                out[both] = g.astype(bf16)
            for hp in range(2):
                b = b0 + hp
                self.leave(b, hp)

                @pl.when(i == 0)
                def _():
                    self.far_b(b, hp)

                @pl.when(i == 2 - hp)
                def _():
                    self.near_b(b, hp)

        def gradient_rest(self):
            g = jnp.dot(
                dl[...].reshape(2048, 1024), rows[:, self.a : self.a + 2 * self.w], preferred_element_type=f32
            ).reshape(8, 256, 2 * self.w)
            eb[:, :, self.a : self.a + 2 * self.w] = g
            self.ga[...] = g[:, :, : self.w].astype(bf16)
            self.gb[...] = g[:, :, self.w :].astype(bf16)
            for hp in range(2):
                s = 1 - 2 * hp
                self.far_b(((y + 2) % 4) * 2 + hp, hp)
                self.near_b(((y - s + 4) % 4) * 2 + hp, hp)
            for b in range(8):
                self.leave(b, b % 2)

        def leave(self, b, hp):
            s = 1 - 2 * hp
            self.send(self.ga.at[b, head(2)], self.ra2.at[b], A2 + b, xd(s)).start()
            self.send(self.ga.at[b, head(-s)], self.ra1m.at[b], A1M + b, xd(-s)).start()

        def far_b(self, b, hp):
            self.send(self.gb.at[b], self.rb2.at[hp], B2 + hp, yd(1 - 2 * hp)).start()

        def near_b(self, b, hp):
            self.send(self.gb.at[b], self.rb1m.at[hp], B1M + hp, yd(2 * hp - 1)).start()

        def ride(self):
            for hp in range(2):
                s = 1 - 2 * hp
                b = ((y + s + 4) % 4) * 2 + hp
                self.send(self.sab.at[hp], self.rb2.at[hp], B2 + hp, yd(s)).wait_recv()
                for r in range(4):
                    at = slice(r * 64, (r + 1) * 64)
                    self.sab[hp, at, :] = (
                        eb[b, at, self.b : self.b + self.w] + self.rb2[hp, at, :].astype(f32)
                    ).astype(bf16)
                self.send(self.sab.at[hp], self.rb1a.at[hp], B1A + hp, yd(s)).start()

            @pl.loop(0, 8)
            def _(b):
                s = 1 - 2 * (b % 2)
                self.send(self.saa.at[b], self.ra2.at[b], A2 + b, xd(s)).wait_recv()
                self.saa[b] = (eb[b, head(s), self.a : self.a + self.w] + self.ra2[b].astype(f32)).astype(bf16)
                self.send(self.saa.at[b], self.ra1a.at[b], A1A + b, xd(s)).start()

        def first(self):
            for hp in range(2):
                s = 1 - 2 * hp
                self.send(self.sab.at[hp], self.rb1m.at[hp], B1M + hp, yd(-s)).wait_recv()
                self.send(self.sab.at[hp], self.rb1a.at[hp], B1A + hp, yd(s)).wait_recv()
                for r in range(4):
                    at = slice(r * 64, (r + 1) * 64)
                    self.sb[hp, at, :] = (
                        eb[y * 2 + hp, at, self.b : self.b + self.w]
                        + self.rb1m[hp, at, :].astype(f32)
                        + self.rb1a[hp, at, :].astype(f32)
                    )
            for d in (2, 1, 3):
                self.s2b[d - 1] = self.sb[:, head(d), :].astype(bf16)
                self.send(self.s2b.at[d - 1], self.r2b.at[d - 1], S2B + d - 1, xd(d)).start()

            @pl.loop(0, 8)
            def _(b):
                s = 1 - 2 * (b % 2)
                self.send(self.saa.at[b], self.ra1m.at[b], A1M + b, xd(-s)).wait_recv()
                self.send(self.saa.at[b], self.ra1a.at[b], A1A + b, xd(s)).wait_recv()
                self.sa[b] = (
                    eb[b, my_head, self.a : self.a + self.w] + self.ra1m[b].astype(f32) + self.ra1a[b].astype(f32)
                )

            for d in (2, 1, 3):
                self.s2a[d - 1] = self.sa[pl.ds(((y + d) % 4) * 2, 2)].astype(bf16)
                self.send(self.s2a.at[d - 1], self.r2a.at[d - 1], S2A + d - 1, yd(d)).start()

        def second(self):
            w = self.w
            for d in range(3):
                self.send(self.s2b.at[d], self.r2b.at[d], S2B + d, xd(d + 1)).wait_recv()
            self.tt[:, :, w:] = (
                self.sb[:, my_head, :]
                + self.r2b[0].astype(f32) + self.r2b[1].astype(f32) + self.r2b[2].astype(f32)
            )
            for d in range(3):
                self.send(self.s2a.at[d], self.r2a.at[d], S2A + d, yd(d + 1)).wait_recv()
            self.tt[:, :, :w] = (
                self.sa[pl.ds(y * 2, 2)]
                + self.r2a[0].astype(f32) + self.r2a[1].astype(f32) + self.r2a[2].astype(f32)
            )
            self.s3[...] = self.tt[...].astype(bf16)
            for d in (4, 3, 5, 2, 6, 1, 7):
                to = (z + d) % 8
                at = pl.ds(pl.multiple_of((to % 4) * 16, 16), 16)
                self.send(self.s3.at[to // 4, at], self.r3.at[d - 1], S3 + d - 1, zd(d)).start()

        def z_share(self, d):
            here = self.fin.at[x, strip]
            return self.send(here, here, GZ + d - 1, dev(x, y, h * 4 + (j + d) % 4))

        def x_share(self, e, d):
            here = self.fin.at[x, pl.ds(pl.multiple_of(((j + 4 - e) % 4) * 16, 16), 16)]
            return self.send(here, here, GX + 3 * e + d - 1, xd(d))

        def third(self):
            total = self.tt[h, strip, :]
            for d in (1, 7, 2, 6, 3, 5, 4):
                self.send(self.r3.at[d - 1], self.r3.at[d - 1], S3 + d - 1, zd(d)).wait_recv()
                total = total + self.r3[d - 1].astype(f32)
            self.fin[x, strip, :] = total.astype(bf16)
            for d in (2, 1, 3):
                self.z_share(d).start()
            for d in (2, 1, 3):
                self.x_share(0, d).start()

        def share(self):
            for e in (1, 3, 2):
                self.z_share(e).wait_recv()
                for d in (2, 1, 3):
                    self.x_share(e, d).start()
            self.store(x)

        def store(self, k):
            grad_out[k, :, self.a : self.a + self.w] = self.fin[k, :, : self.w]
            grad_out[k, :, self.b : self.b + self.w] = self.fin[k, :, self.w :]

        def finish(self):
            for d in (1, 3, 2):
                for e in (0, 1, 3, 2):
                    self.x_share(e, d).wait_recv()
                self.store((x + 4 - d) % 4)

        def sent(self):
            for b in range(8):
                for sem in (A2, A1M, A1A):
                    self.send(self.saa.at[b], self.ra2.at[b], sem + b, sib).wait_send()
            for hp in range(2):
                for sem in (B2, B1M, B1A):
                    self.send(self.sab.at[hp], self.rb2.at[hp], sem + hp, sib).wait_send()
            for d in range(3):
                self.send(self.s2a.at[d], self.r2a.at[d], S2A + d, sib).wait_send()
                self.send(self.s2b.at[d], self.r2b.at[d], S2B + d, sib).wait_send()
                self.z_share(d + 1).wait_send()
                for e in range(4):
                    self.x_share(e, d + 1).wait_send()
            for d in range(7):
                self.send(self.r3.at[d], self.r3.at[d], S3 + d, sib).wait_send()

    one, two = Part(0), Part(1)

    @pl.loop(0, 4)
    def _(i):
        one.gradient(i)

    two.gradient_rest()

    one.ride()
    two.ride()
    one.first()
    two.first()
    one.second()
    two.second()
    one.third()
    two.third()
    one.share()
    two.share()
    one.finish()
    two.finish()

    for m in range(2):
        for sem, count in ((Y_C, 128), (Y_C + 1, 128)):
            move(m, 0, 0, count, sem, yd(1)).wait_send()
        for sem in (Y2, Y2 + 1):
            move(m, 0, 0, 64, sem, yd(1)).wait_send()
        for sem in range(ZU, XQ):
            move(m, 0, 0, 16, sem, yd(1)).wait_send()
        for sem in range(XQ, GATHER):
            move(m, 0, 0, 32, sem, yd(1)).wait_send()
    for role in range(8):
        to_sibling(role).wait_send()
    row_copy.wait_send()
    id_copy.wait_send()
    one.sent()
    two.sent()


def widen(loss, grad, loss_out, grad_out):
    loss_out[...] = loss[...]
    grad_out[...] = grad[...].astype(f32)


def part_scratch(w):
    shapes = (
        [((8, 256, w), bf16)] * 2 + [((8, 64, w), bf16)] * 4 + [((2, 256, w), bf16)] * 4
        + [((8, 64, w), f32), ((2, 256, w), f32)] + [((3, 2, 64, w), bf16)] * 4
        + [((2, 64, 2 * w), f32), ((2, 64, 2 * w), bf16), ((7, 16, 2 * w), bf16), ((4, 64, 2 * w), bf16)]
    )
    return [pltpu.VMEM(shape, kind) for shape, kind in shapes]


def shards(hidden, temporal_gain, in_weight, in_scale, depth_gain, head_weight, code_ids):
    vmem = pl.BlockSpec(memory_space=pltpu.VMEM)
    hbm = pl.BlockSpec(memory_space=pl.ANY)
    V = pltpu.VMEM
    loss, grad = pl.pallas_call(
        kernel,
        out_shape=(jax.ShapeDtypeStruct((4, 512), f32), jax.ShapeDtypeStruct((4, 64, 1024), bf16)),
        in_specs=[hbm, vmem, hbm, vmem, vmem, hbm, vmem],
        out_specs=(vmem, vmem),
        scratch_shapes=[
            V((256, 1024), bf16), V((512, 4096), bf16), V((8, 2, 512, 256), bf16), V((2, 8, 256, 1024), bf16), V((8, 256, 1024), bf16),
            V((512, 1024), f32), V((1024, 1024), bf16), V((8, 256, 1024), f32), V((8, 256, 1024), f32),
            V((8, 256, 1024), bf16), V((2, 4, 512), jnp.int32), V((2, 8, 1024), f32),
            pltpu.SemaphoreType.DMA((3,)), pltpu.SemaphoreType.DMA((N_SEM,)), pltpu.SemaphoreType.DMA((N_SEM,)),
            *part_scratch(WIDTH[0]), *part_scratch(WIDTH[1]),
        ],
        compiler_params=pltpu.CompilerParams(
            collective_id=0, has_side_effects=True, vmem_limit_bytes=63 * 2**20
        ),
    )(
        hidden, temporal_gain[None, :], in_weight, in_scale, depth_gain[None, :],
        head_weight.reshape(256, 1024), code_ids.T,
    )
    loss, grad = pl.pallas_call(
        widen,
        out_shape=(jax.ShapeDtypeStruct((4, 512), f32), jax.ShapeDtypeStruct((4, 64, 1024), f32)),
        in_specs=[vmem, vmem],
        out_specs=(vmem, vmem),
    )(loss, grad)
    return loss.T, grad


def solution(mesh):
    in_specs = (
        P(("dp", "fsdp"), None),
        P(),
        P("fsdp", None),
        P("fsdp"),
        P(),
        P(None, "fsdp", None),
        P(("dp", "fsdp"), None),
    )
    out_specs = (P(("dp", "fsdp"), None), P(None, "fsdp", None))
    return jax.shard_map(shards, mesh=mesh, in_specs=in_specs, out_specs=out_specs, check_vma=False)
```

```python
import functools

import jax
import jax.numpy as jnp
from jax import lax
from jax.experimental import pallas as pl
from jax.experimental.pallas import tpu as pltpu
from jax.sharding import PartitionSpec as P

MESH = pl.DeviceIdType.MESH
f32, bf16 = jnp.float32, jnp.bfloat16
eps = 1e-05
cap = 30.0
loss_scale = 0.0625

Y_A, Y_B, Y_C, Y2, ZU, ZD, XQ = 0, 2, 4, 6, 8, 24, 40
GATHER = 60
SIB_W, SIB_R, SIB_S, SIB_I = 120, 128, 129, 130
RS = 131
A2, A1M, A1A, B2, B1M, B1A, S2A, S2B, S3, GZ, GX = 0, 8, 16, 24, 26, 28, 30, 33, 36, 43, 46
SUM = 58
N_SEM = RS + 2 * SUM
HOP = 4
WIDTH = (256, 256)
A_COL = (0, WIDTH[0])
B_COL = (1024 - WIDTH[0], WIDTH[0] + WIDTH[1])


def kernel(
    hidden, t_gain, weight, scale, d_gain, heads, ids,
    loss_out, grad_out,
    wbuf, hid, normed, pg, ws, acc, rows, tb, eb, dl, idb, sums, lsem, ss, rs, *parts,
):
    half_parts = len(parts) // 2
    parts = (parts[:half_parts], parts[half_parts:])
    dp, fs = lax.axis_index("dp"), lax.axis_index("fsdp")
    x, y, c = dp % 4, fs // 4, fs % 2
    h, j = (fs // 2) % 2, dp // 4
    z = h * 4 + j
    par = x % 2

    def dev(px, py, pz, pc=None):
        px, py, pz = (px + 4) % 4, (py + 4) % 4, (pz + 8) % 8
        return {"dp": (pz % 4) * 4 + px, "fsdp": (py * 2 + pz // 4) * 2 + (c if pc is None else pc)}

    sib = dev(x, y, z, 1 - c)
    xd = lambda d: dev(x + d, y, z)
    yd = lambda d: dev(x, y + d, z)
    zd = lambda d: dev(x, y, z + d)

    def copy(src, dst, sem, to):
        return pltpu.make_async_remote_copy(
            src_ref=src, dst_ref=dst, send_sem=ss.at[sem], recv_sem=rs.at[sem], device_id=to, device_id_type=MESH
        )

    barrier = pltpu.get_barrier_semaphore()
    everyone = [sib] + [xd(d) for d in (1, 2, 3)] + [yd(d) for d in (1, 2, 3)] + [zd(d) for d in range(1, 8)]
    for to in everyone:
        pl.semaphore_signal(barrier, inc=1, device_id=to, device_id_type=MESH)

    weight_copy = pltpu.make_async_copy(weight, wbuf, lsem.at[2])
    weight_copy.start()
    hid_copy = pltpu.make_async_copy(hidden, hid, lsem.at[0])
    hid_copy.start()
    own = y * 2 + h
    head_copy = pltpu.make_async_copy(heads, pg.at[1, own], lsem.at[1])
    head_copy.start()

    on_diagonal = lax.broadcasted_iota(jnp.int32, (256, 256), 0) == lax.broadcasted_iota(jnp.int32, (256, 256), 1)
    diagonal = jnp.where(on_diagonal, scale[...].astype(f32)[None, :], 0.0).astype(bf16)
    weight_copy.wait()
    pg[0, own] = jnp.dot(diagonal, wbuf[...], preferred_element_type=f32).astype(bf16)
    idb[pl.ds(c, 1)] = ids[...][None]
    pl.semaphore_wait(barrier, len(everyone))

    def slot(role):
        off = jnp.where(role % 4 == 1, 3, jnp.where(role % 4 == 2, 1, jnp.where(role % 4 == 3, 2, 0)))
        return ((y + off) % 4) * 2 + jnp.where(role < 4, h, 1 - h)

    def piece(m, role, start, count):
        return pg.at[m, slot(role), pl.ds(pl.multiple_of(start, 16), count)]

    q0, q1, rest = par * 128, par * 128 + 64, (1 - par) * 128
    o0, o1 = (1 - par) * 128, (1 - par) * 128 + 64

    def move(m, role, start, count, sem, to):
        ref = piece(m, role, start, count)
        return copy(ref, ref, m * GATHER + sem, to)

    def y_send(m, sem):
        plus, minus, count = {Y_A: (q0, q1, 64), Y_B: (q1, q0, 64), Y_C: (rest, rest, 128)}[sem]
        move(m, 0, plus, count, sem, yd(1)).start()
        move(m, 0, minus, count, sem + 1, yd(-1)).start()

    def z_up(m, k, sub):
        return move(m, k, q0 + 16 * sub, 16, ZU + 4 * (k % 4) + sub, zd(1))

    def z_down(m, k, sub):
        return move(m, k, q1 + 16 * sub, 16, ZD + 4 * (k % 4) + sub, zd(-1))

    def y_sent(m, sem):
        move(m, 0, 0, 64, sem, yd(1)).wait_send()
        move(m, 0, 0, 64, sem + 1, yd(-1)).wait_send()

    def up_source(m, k):
        @pl.when(j == 3)
        def _():
            for sub in range(4):
                z_up(m, k, sub).start()

    def down_source(m, k):
        @pl.when(j == 0)
        def _():
            for sub in range(4):
                z_down(m, k, sub).start()

    def x_up(m, role, half):
        return move(m, role, q0 + 32 * half, 32, XQ + 4 * (role - 3) + 2 * half, xd(1))

    def x_down(m, role, half):
        return move(m, role, q1 + 32 * half, 32, XQ + 4 * (role - 3) + 2 * half + 1, xd(-1))

    def y_first(m):
        move(m, 1, q0, 64, Y_A, yd(1)).wait_recv()
        move(m, 1, q0, 64, Y2, yd(1)).start()
        up_source(m, 1)
        move(m, 2, q1, 64, Y_A + 1, yd(-1)).wait_recv()
        move(m, 2, q1, 64, Y2 + 1, yd(-1)).start()
        down_source(m, 2)

    def y_second(m):
        move(m, 1, q1, 64, Y_B, yd(1)).wait_recv()
        down_source(m, 1)
        move(m, 2, q0, 64, Y_B + 1, yd(-1)).wait_recv()
        up_source(m, 2)

    def y_rest(m):
        move(m, 1, rest, 128, Y_C, yd(1)).wait_recv()
        move(m, 2, rest, 128, Y_C + 1, yd(-1)).wait_recv()

    def y_far(m):
        move(m, 3, q0, 64, Y2, yd(1)).wait_recv()
        up_source(m, 3)
        x_up(m, 3, 0).start()
        x_up(m, 3, 1).start()
        move(m, 3, q1, 64, Y2 + 1, yd(-1)).wait_recv()
        down_source(m, 3)
        x_down(m, 3, 0).start()
        x_down(m, 3, 1).start()

    def z_piece(i, first):
        q = i // 4
        k = jnp.where(q < 2, 0, jnp.where(q < 5, q - 1, q - 4))
        k = jnp.where(k == 1, first, jnp.where(k == 2, 3 - first, k))
        return jnp.where(jnp.logical_or(q == 1, q >= 5), 1, 0), 4 + k, i % 4

    def z_one(n):
        up, down = n - HOP * j, n - HOP * (3 - j)

        @pl.when(jnp.logical_and(up >= 0, up < 32))
        def _():
            m, role, sub = z_piece(up, 1)
            z_up(m, role, sub).wait_recv()

            @pl.when(j < 3)
            def _():
                z_up(m, role, sub).start()

            @pl.when(sub % 2 == 1)
            def _():
                x_up(m, role, sub // 2).start()

        @pl.when(jnp.logical_and(down >= 0, down < 32))
        def _():
            m, role, sub = z_piece(down, 2)
            z_down(m, role, sub).wait_recv()

            @pl.when(j > 0)
            def _():
                z_down(m, role, sub).start()

            @pl.when(sub % 2 == 1)
            def _():
                x_down(m, role, sub // 2).start()

    def z_step(n):
        @pl.loop(2 * n, 2 * n + 2)
        def _(i):
            z_one(i)

    def x_wait(m, role):
        for half in range(2):
            sem = XQ + 4 * (role - 3) + 2 * half
            move(m, role, o0 + 32 * half, 32, sem, xd(1)).wait_recv()
            move(m, role, o1 + 32 * half, 32, sem + 1, xd(-1)).wait_recv()

    def to_sibling(role):
        s = slot(role)
        return copy(pg.at[0, s], ws.at[s], SIB_W + role, sib)

    def project(role):
        to_sibling(role).wait_recv()
        s = slot(role)

        acc[...] += jnp.dot(normed[s, c], pg[0, s], preferred_element_type=f32) + jnp.dot(
            normed[s, 1 - c], ws[s], preferred_element_type=f32
        )

    y_send(0, Y_A)
    up_source(0, 0)
    down_source(0, 0)
    to_sibling(0).start()
    id_copy = copy(idb.at[c], idb.at[c], SIB_I, sib)
    id_copy.start()
    head_copy.wait()
    up_source(1, 0)
    down_source(1, 0)
    acc[...] = jnp.zeros_like(acc)
    sums[...] = jnp.zeros_like(sums)
    hid_copy.wait()

    def norm(part):
        at = pl.ds(part * 64, 64)
        block = hid[at, :].astype(f32)
        inv = lax.rsqrt(jnp.mean(block * block, axis=-1, keepdims=True) + eps)
        out = (block * inv * t_gain[...]).astype(bf16)
        for s in range(16):
            normed[s // 2, s % 2, at, :] = out[:, s * 256 : (s + 1) * 256]

    norm(0)
    norm(1)
    y_sent(0, Y_A)
    y_send(0, Y_B)
    z_step(0)
    y_first(0)
    z_step(1)
    norm(2)
    z_step(2)
    y_sent(0, Y_B)
    y_send(1, Y_A)
    z_step(3)
    y_second(0)
    z_step(4)
    norm(3)
    z_step(5)
    y_far(0)
    y_sent(1, Y_A)
    y_send(1, Y_B)
    z_step(6)
    y_first(1)
    norm(4)
    z_step(7)
    z_step(8)
    y_sent(1, Y_B)
    y_second(1)
    norm(5)
    z_step(9)
    z_step(10)
    y_far(1)
    y_send(0, Y_C)
    norm(6)
    z_step(11)
    norm(7)
    z_step(12)
    z_step(13)
    x_wait(0, 3)
    to_sibling(3).start()
    project(0)
    z_step(14)
    x_wait(0, 4)
    to_sibling(4).start()
    z_step(15)
    project(3)
    y_send(1, Y_C)
    z_step(16)
    project(4)
    z_step(17)
    z_step(18)
    y_rest(0)
    to_sibling(1).start()
    to_sibling(2).start()
    z_step(19)
    x_wait(0, 5)
    to_sibling(5).start()
    project(1)
    x_wait(0, 6)
    to_sibling(6).start()
    z_step(20)
    project(2)
    project(5)
    z_step(21)
    project(6)
    x_wait(0, 7)
    to_sibling(7).start()
    project(7)

    @pl.loop(0, 2)
    def _(r):
        block = acc[pl.ds(pl.multiple_of(r * 256, 256), 256), :]
        inv = lax.rsqrt(jnp.mean(block * block, axis=-1, keepdims=True) + eps)
        rows[pl.ds(pl.multiple_of(c * 512 + r * 256, 256), 256), :] = (block * inv * d_gain[...]).astype(bf16)

    my_rows = rows.at[pl.ds(pl.multiple_of(c * 512, 512), 512)]
    row_copy = copy(my_rows, my_rows, SIB_R, sib)
    row_copy.start()
    id_copy.wait_recv()
    y_rest(1)
    for role in range(3, 8):
        x_wait(1, role)

    def score(n):
        cols = pl.ds(pl.multiple_of(n * 256, 256), 256)
        ids_at = idb[n // 2, :, pl.ds(pl.multiple_of((n % 2) * 256, 256), 256)]
        total, target = [0.0] * 4, [0.0] * 4
        for b in range(8):
            got = lax.dot_general(
                pg[1, b], rows[cols, :], (((1,), (1,)), ((), ())), preferred_element_type=f32
            )
            card = lax.broadcasted_iota(jnp.int32, (64, 256), 0) + (b * 2 + c) * 64
            for k in range(4):
                part = slice(k * 64, (k + 1) * 64)
                t = jnp.tanh(got[part] * (1.0 / cap))
                e = jnp.exp(t * cap)
                tb[b, part, cols] = t
                eb[b, part, cols] = e
                hit = card == ids_at[k : k + 1, :]
                total[k] += jnp.sum(e.reshape(8, 8, 256), axis=0)
                target[k] += jnp.sum(jnp.where(hit, t, 0.0).reshape(8, 8, 256), axis=0)
        for k in range(4):
            sums[c, k : k + 1, cols] = jnp.sum(total[k], axis=0, keepdims=True)
            sums[c, k + 4 : k + 5, cols] = jnp.sum(target[k], axis=0, keepdims=True)

    @pl.loop(0, 2)
    def _(n):
        score(c * 2 + n)

    row_copy.wait_recv()

    @pl.loop(0, 2)
    def _(n):
        score((1 - c) * 2 + n)

    my_sums = sums.at[c]
    sum_copy = copy(my_sums, my_sums, SIB_S, sib)
    sum_copy.start()
    sum_copy.wait_recv()
    totals = sums[0, 0:4, :] + sums[1, 0:4, :]
    mine_f = pl.ds(pl.multiple_of(c * 512, 512), 512)
    loss_out[...] = jnp.log(sums[0, 0:4, mine_f] + sums[1, 0:4, mine_f]) - cap * (
        sums[0, 4:8, mine_f] + sums[1, 4:8, mine_f]
    )
    sum_copy.wait_send()
    sums[c, 0:4, :] = 1.0 / totals

    def logits(b):
        @pl.loop(0, 4)
        def _(n):
            cols = pl.ds(pl.multiple_of(n * 256, 256), 256)
            ids_at = idb[n // 2, :, pl.ds(pl.multiple_of((n % 2) * 256, 256), 256)]
            card = lax.broadcasted_iota(jnp.int32, (64, 256), 0) + (b * 2 + c) * 64
            for k in range(4):
                part = slice(k * 64, (k + 1) * 64)
                t = tb[b, part, cols]
                p = eb[b, part, cols] * sums[c, k : k + 1, cols]
                hit = card == ids_at[k : k + 1, :]
                p = jnp.where(hit, p - 1.0, p)
                dl[b, part, cols] = (p * ((1.0 - t * t) * loss_scale)).astype(bf16)

    head = lambda d: pl.ds(pl.multiple_of(((x + d + 4) % 4) * 64, 64), 64)
    my_head = head(0)
    strip = pl.ds(pl.multiple_of(j * 16, 16), 16)

    class Part:
        def __init__(self, q):
            self.w, self.a, self.b, self.base = WIDTH[q], A_COL[q], B_COL[q], RS + q * SUM
            (self.ga, self.gb, self.ra2, self.ra1m, self.ra1a, self.saa, self.rb2, self.rb1m, self.rb1a, self.sab,
             self.sa, self.sb, self.s2a, self.r2a, self.s2b, self.r2b, self.tt, self.s3, self.r3, self.fin) = parts[q]

        def send(self, src, dst, sem, to):
            return copy(src, dst, self.base + sem, to)

        def gradient(self, i):
            b0 = ((y + jnp.where(i == 0, 2, jnp.where(i == 1, 1, jnp.where(i == 2, 3, 0)))) % 4) * 2
            logits(b0)
            logits(b0 + 1)
            both = pl.ds(b0, 2)
            for col, out in ((self.a, self.ga), (self.b, self.gb)):
                g = jnp.dot(
                    dl[both].reshape(512, 1024), rows[:, col : col + self.w], preferred_element_type=f32
                ).reshape(2, 256, self.w)
                eb[both, :, col : col + self.w] = g
                out[both] = g.astype(bf16)
            for hp in range(2):
                b = b0 + hp
                self.leave(b, hp)

                @pl.when(i == 0)
                def _():
                    self.far_b(b, hp)

                @pl.when(i == 2 - hp)
                def _():
                    self.near_b(b, hp)

        def gradient_rest(self):
            g = jnp.dot(
                dl[...].reshape(2048, 1024), rows[:, self.a : self.a + 2 * self.w], preferred_element_type=f32
            ).reshape(8, 256, 2 * self.w)
            eb[:, :, self.a : self.a + 2 * self.w] = g
            self.ga[...] = g[:, :, : self.w].astype(bf16)
            self.gb[...] = g[:, :, self.w :].astype(bf16)
            for hp in range(2):
                s = 1 - 2 * hp
                self.far_b(((y + 2) % 4) * 2 + hp, hp)
                self.near_b(((y - s + 4) % 4) * 2 + hp, hp)
            for b in range(8):
                self.leave(b, b % 2)

        def leave(self, b, hp):
            s = 1 - 2 * hp
            self.send(self.ga.at[b, head(2)], self.ra2.at[b], A2 + b, xd(s)).start()
            self.send(self.ga.at[b, head(-s)], self.ra1m.at[b], A1M + b, xd(-s)).start()

        def far_b(self, b, hp):
            self.send(self.gb.at[b], self.rb2.at[hp], B2 + hp, yd(1 - 2 * hp)).start()

        def near_b(self, b, hp):
            self.send(self.gb.at[b], self.rb1m.at[hp], B1M + hp, yd(2 * hp - 1)).start()

        def ride(self):
            for hp in range(2):
                s = 1 - 2 * hp
                b = ((y + s + 4) % 4) * 2 + hp
                self.send(self.sab.at[hp], self.rb2.at[hp], B2 + hp, yd(s)).wait_recv()
                for r in range(4):
                    at = slice(r * 64, (r + 1) * 64)
                    self.sab[hp, at, :] = (
                        eb[b, at, self.b : self.b + self.w] + self.rb2[hp, at, :].astype(f32)
                    ).astype(bf16)
                self.send(self.sab.at[hp], self.rb1a.at[hp], B1A + hp, yd(s)).start()

            @pl.loop(0, 8)
            def _(b):
                s = 1 - 2 * (b % 2)
                self.send(self.saa.at[b], self.ra2.at[b], A2 + b, xd(s)).wait_recv()
                self.saa[b] = (eb[b, head(s), self.a : self.a + self.w] + self.ra2[b].astype(f32)).astype(bf16)
                self.send(self.saa.at[b], self.ra1a.at[b], A1A + b, xd(s)).start()

        def first(self):
            for hp in range(2):
                s = 1 - 2 * hp
                self.send(self.sab.at[hp], self.rb1m.at[hp], B1M + hp, yd(-s)).wait_recv()
                self.send(self.sab.at[hp], self.rb1a.at[hp], B1A + hp, yd(s)).wait_recv()
                for r in range(4):
                    at = slice(r * 64, (r + 1) * 64)
                    self.sb[hp, at, :] = (
                        eb[y * 2 + hp, at, self.b : self.b + self.w]
                        + self.rb1m[hp, at, :].astype(f32)
                        + self.rb1a[hp, at, :].astype(f32)
                    )
            for d in (2, 1, 3):
                self.s2b[d - 1] = self.sb[:, head(d), :].astype(bf16)
                self.send(self.s2b.at[d - 1], self.r2b.at[d - 1], S2B + d - 1, xd(d)).start()

            @pl.loop(0, 8)
            def _(b):
                s = 1 - 2 * (b % 2)
                self.send(self.saa.at[b], self.ra1m.at[b], A1M + b, xd(-s)).wait_recv()
                self.send(self.saa.at[b], self.ra1a.at[b], A1A + b, xd(s)).wait_recv()
                self.sa[b] = (
                    eb[b, my_head, self.a : self.a + self.w] + self.ra1m[b].astype(f32) + self.ra1a[b].astype(f32)
                )

            for d in (2, 1, 3):
                self.s2a[d - 1] = self.sa[pl.ds(((y + d) % 4) * 2, 2)].astype(bf16)
                self.send(self.s2a.at[d - 1], self.r2a.at[d - 1], S2A + d - 1, yd(d)).start()

        def second(self):
            w = self.w
            for d in range(3):
                self.send(self.s2b.at[d], self.r2b.at[d], S2B + d, xd(d + 1)).wait_recv()
            self.tt[:, :, w:] = (
                self.sb[:, my_head, :]
                + self.r2b[0].astype(f32) + self.r2b[1].astype(f32) + self.r2b[2].astype(f32)
            )
            for d in range(3):
                self.send(self.s2a.at[d], self.r2a.at[d], S2A + d, yd(d + 1)).wait_recv()
            self.tt[:, :, :w] = (
                self.sa[pl.ds(y * 2, 2)]
                + self.r2a[0].astype(f32) + self.r2a[1].astype(f32) + self.r2a[2].astype(f32)
            )
            self.s3[...] = self.tt[...].astype(bf16)
            for d in (4, 3, 5, 2, 6, 1, 7):
                to = (z + d) % 8
                at = pl.ds(pl.multiple_of((to % 4) * 16, 16), 16)
                self.send(self.s3.at[to // 4, at], self.r3.at[d - 1], S3 + d - 1, zd(d)).start()

        def z_share(self, d):
            here = self.fin.at[x, strip]
            return self.send(here, here, GZ + d - 1, dev(x, y, h * 4 + (j + d) % 4))

        def x_share(self, e, d):
            here = self.fin.at[x, pl.ds(pl.multiple_of(((j + 4 - e) % 4) * 16, 16), 16)]
            return self.send(here, here, GX + 3 * e + d - 1, xd(d))

        def third(self):
            total = self.tt[h, strip, :]
            for d in (1, 7, 2, 6, 3, 5, 4):
                self.send(self.r3.at[d - 1], self.r3.at[d - 1], S3 + d - 1, zd(d)).wait_recv()
                total = total + self.r3[d - 1].astype(f32)
            self.fin[x, strip, :] = total.astype(bf16)
            for d in (2, 1, 3):
                self.z_share(d).start()
            for d in (2, 1, 3):
                self.x_share(0, d).start()

        def share(self):
            for e in (1, 3, 2):
                self.z_share(e).wait_recv()
                for d in (2, 1, 3):
                    self.x_share(e, d).start()
            self.store(x)

        def store(self, k):
            grad_out[k, :, self.a : self.a + self.w] = self.fin[k, :, : self.w]
            grad_out[k, :, self.b : self.b + self.w] = self.fin[k, :, self.w :]

        def finish(self):
            for d in (1, 3, 2):
                for e in (0, 1, 3, 2):
                    self.x_share(e, d).wait_recv()
                self.store((x + 4 - d) % 4)

        def sent(self):
            for b in range(8):
                for sem in (A2, A1M, A1A):
                    self.send(self.saa.at[b], self.ra2.at[b], sem + b, sib).wait_send()
            for hp in range(2):
                for sem in (B2, B1M, B1A):
                    self.send(self.sab.at[hp], self.rb2.at[hp], sem + hp, sib).wait_send()
            for d in range(3):
                self.send(self.s2a.at[d], self.r2a.at[d], S2A + d, sib).wait_send()
                self.send(self.s2b.at[d], self.r2b.at[d], S2B + d, sib).wait_send()
                self.z_share(d + 1).wait_send()
                for e in range(4):
                    self.x_share(e, d + 1).wait_send()
            for d in range(7):
                self.send(self.r3.at[d], self.r3.at[d], S3 + d, sib).wait_send()

    one, two = Part(0), Part(1)

    @pl.loop(0, 4)
    def _(i):
        one.gradient(i)

    two.gradient_rest()

    one.ride()
    two.ride()
    one.first()
    two.first()
    one.second()
    two.second()
    one.third()
    two.third()
    one.share()
    two.share()
    one.finish()
    two.finish()

    for m in range(2):
        for sem, count in ((Y_C, 128), (Y_C + 1, 128)):
            move(m, 0, 0, count, sem, yd(1)).wait_send()
        for sem in (Y2, Y2 + 1):
            move(m, 0, 0, 64, sem, yd(1)).wait_send()
        for sem in range(ZU, XQ):
            move(m, 0, 0, 16, sem, yd(1)).wait_send()
        for sem in range(XQ, GATHER):
            move(m, 0, 0, 32, sem, yd(1)).wait_send()
    for role in range(8):
        to_sibling(role).wait_send()
    row_copy.wait_send()
    id_copy.wait_send()
    one.sent()
    two.sent()


def widen(loss, grad, loss_out, grad_out):
    loss_out[...] = loss[...]
    grad_out[...] = grad[...].astype(f32)


def part_scratch(w):
    shapes = (
        [((8, 256, w), bf16)] * 2 + [((8, 64, w), bf16)] * 4 + [((2, 256, w), bf16)] * 4
        + [((8, 64, w), f32), ((2, 256, w), f32)] + [((3, 2, 64, w), bf16)] * 4
        + [((2, 64, 2 * w), f32), ((2, 64, 2 * w), bf16), ((7, 16, 2 * w), bf16), ((4, 64, 2 * w), bf16)]
    )
    return [pltpu.VMEM(shape, kind) for shape, kind in shapes]


def shards(hidden, temporal_gain, in_weight, in_scale, depth_gain, head_weight, code_ids):
    vmem = pl.BlockSpec(memory_space=pltpu.VMEM)
    hbm = pl.BlockSpec(memory_space=pl.ANY)
    V = pltpu.VMEM
    loss, grad = pl.pallas_call(
        kernel,
        out_shape=(jax.ShapeDtypeStruct((4, 512), f32), jax.ShapeDtypeStruct((4, 64, 1024), bf16)),
        in_specs=[hbm, vmem, hbm, vmem, vmem, hbm, vmem],
        out_specs=(vmem, vmem),
        scratch_shapes=[
            V((256, 1024), bf16), V((512, 4096), bf16), V((8, 2, 512, 256), bf16), V((2, 8, 256, 1024), bf16), V((8, 256, 1024), bf16),
            V((512, 1024), f32), V((1024, 1024), bf16), V((8, 256, 1024), f32), V((8, 256, 1024), f32),
            V((8, 256, 1024), bf16), V((2, 4, 512), jnp.int32), V((2, 8, 1024), f32),
            pltpu.SemaphoreType.DMA((3,)), pltpu.SemaphoreType.DMA((N_SEM,)), pltpu.SemaphoreType.DMA((N_SEM,)),
            *part_scratch(WIDTH[0]), *part_scratch(WIDTH[1]),
        ],
        compiler_params=pltpu.CompilerParams(
            collective_id=0, has_side_effects=True, vmem_limit_bytes=63 * 2**20
        ),
    )(
        hidden, temporal_gain[None, :], in_weight, in_scale, depth_gain[None, :],
        head_weight.reshape(256, 1024), code_ids.T,
    )
    loss, grad = pl.pallas_call(
        widen,
        out_shape=(jax.ShapeDtypeStruct((4, 512), f32), jax.ShapeDtypeStruct((4, 64, 1024), f32)),
        in_specs=[vmem, vmem],
        out_specs=(vmem, vmem),
    )(loss, grad)
    return loss.T, grad


def solution(mesh):
    in_specs = (
        P(("dp", "fsdp"), None),
        P(),
        P("fsdp", None),
        P("fsdp"),
        P(),
        P(None, "fsdp", None),
        P(("dp", "fsdp"), None),
    )
    out_specs = (P(("dp", "fsdp"), None), P(None, "fsdp", None))
    return jax.shard_map(shards, mesh=mesh, in_specs=in_specs, out_specs=out_specs, check_vma=False)
```
